32 devices in a mesh: ctx: 8 (over y, x, core), tp: 4 (over z).
Axes of the slice: x: 2, y: 2, z: 4, core: 2. Of those that a mesh axis runs over, the one named last changes fastest.
Arguments:
- ssm_input: bfloat16 [2048, 4096], P('ctx', 'tp'), may hold values from -6 to 6
- dt_raw: float32 [2048, 64], P('ctx', 'tp'), may hold values from -5 to 5
- b_proj: bfloat16 [2048, 4, 256], P('ctx', 'tp'), may hold values from -0.59765625 to 0.59765625
- c_proj: bfloat16 [2048, 4, 256], P('ctx', 'tp'), may hold values from -0.59765625 to 0.59765625
- dt_bias: float32 [64], P('tp'), may hold values from -1.5 to 0.5
- decay_rate: float32 [64], P('tp'), may hold values from 0.0002 to 0.05
- skip_gain: float32 [64], P('tp'), may hold values from 0.5 to 1.5
- doc_start: int32 [2048], P('ctx'), may hold values 0 or 1
- out_weight: bfloat16 [4096, 8192], P('tp'), may hold values from -0.09375 to 0.09375
- grad_out: bfloat16 [2048, 8192], P(('ctx', 'tp')), may hold values from -6 to 6
Outputs:
- layer_out: bfloat16 [2048, 8192], P(('ctx', 'tp'))
- grad_input: bfloat16 [2048, 4096], P('ctx', 'tp')
- grad_dt: float32 [2048, 64], P('ctx', 'tp')
- grad_b: bfloat16 [2048, 4, 256], P('ctx', 'tp')
- grad_c: bfloat16 [2048, 4, 256], P('ctx', 'tp')
- weight_grad: bfloat16 [8192, 4096], P('ctx', 'tp')
The draws below stay inside these ranges and needn't reach their ends.
Inputs may be any that keep to these rules, and one draw needn't show every extreme that they name: `doc_start`: 1 marks the first token of a document; a document runs on until the next 1, across slabs.
All inputs are finite; a program needn't handle non-finite values. No bound on the sum of `doc_start` on one device may be relied on, other than what follows from the above.
Results may differ from the reference program's by a relative error of at most 0.022.
Values may be sent and summed in bfloat16 or wider, within the bound.
A program may use at most 256 MiB of HBM per device.

```python
import math
import jax
import jax.numpy as jnp
from jax import lax

WIDTH = 8192
HEADS_DEV = 16
HEAD_DIM = 64
STATE = 256
TOK_DEV = 256
GROUPS = 4
HEADS = 64
INNER = 4096
TOKENS = 2048
N_CTX = 8


def touch_ends(array, rng, smallest, high):
    extent = array.shape
    place = [jax.random.randint(jax.random.fold_in(rng, axis), (), 0, extent[axis]) for axis in range(len(extent))]
    array = array.at[tuple(place)].set(smallest)
    longest = extent.index(max(extent))
    place[longest] = (place[longest] + 1) % extent[longest]
    return array.at[tuple(place)].set(high)


def shard_levels(rng, extent, split, low, top_value):
    level = 1.0
    for axis_at, shards_of in split:
        draws = jax.random.uniform(jax.random.fold_in(jax.random.fold_in(rng, 6), axis_at), (shards_of,), jnp.float32, low / len(split), top_value / len(split))
        level = level * jnp.repeat(jnp.exp(draws), extent[axis_at] // shards_of).reshape((-1,) + (1,) * (len(extent) - 1 - axis_at))
    return level


def centred(key, dims, spread, bound, cuts=(), dtype=jnp.bfloat16):
    factor_of = shard_levels(key, dims, cuts, -0.22, 0.18) if cuts else 1.0
    array = jax.random.normal(key, dims, jnp.float32) * spread * factor_of
    return jnp.minimum(jnp.maximum(array, -bound), bound).astype(dtype)


def setup_inputs(seed: int = 0) -> dict:
    splits = jax.random.split(jax.random.key(seed), 11)
    return {
        "ssm_input": centred(splits[0], (TOKENS, INNER), 1.0, 6.0, ((0, 8), (1, 4))),
        "dt_raw": centred(splits[1], (TOKENS, HEADS), 1.0, 5.0, ((0, 8), (1, 4)), jnp.float32),
        "b_proj": centred(splits[2], (TOKENS, GROUPS, STATE), 0.1, 0.59765625, ((0, 8), (1, 4))),
        "c_proj": centred(splits[3], (TOKENS, GROUPS, STATE), 0.1, 0.59765625, ((0, 8), (1, 4))),
        "dt_bias": jnp.clip(-1.5 + 2.0 * jax.random.uniform(splits[4], (HEADS,), jnp.float32) ** shard_levels(splits[4], (HEADS,), ((0, 4),), -0.2, 0.2), -1.5, 0.5),
        "decay_rate": jnp.clip(jnp.exp(math.log(0.05) - 5.521461 * jax.random.uniform(splits[5], (HEADS,), jnp.float32) ** shard_levels(splits[5], (HEADS,), ((0, 4),), -0.2, 0.2)), 0.0002, 0.05),
        "skip_gain": jnp.clip(1.0 + 0.1 * jax.random.normal(splits[6], (HEADS,), jnp.float32), 0.5, 1.5),
        "doc_start": touch_ends((jax.random.randint(splits[7], (TOKENS,), 0, 4096) < 1).astype(jnp.int32), jax.random.fold_in(splits[7], 1), 0, 1),
        "out_weight": centred(splits[8], (INNER, WIDTH), INNER ** -0.5, 0.09375, ((0, 4),)),
        "grad_out": centred(splits[9], (TOKENS, WIDTH), 1.0, 6.0, ((0, 32),)),
    }


HIGHEST = lax.Precision.HIGHEST

def block_ssd(seq_in, step_raw, b_rows, c_rows, carried, doc_start, bias_heads, rate_heads, skip_heads):
    length = seq_in.shape[0]
    step_size = jax.nn.softplus(step_raw + bias_heads)
    cumul = jnp.cumsum(-step_size * rate_heads, axis=0)
    segment = jnp.cumsum(doc_start)
    reach = (segment == 0).astype(jnp.float32)
    order = jnp.arange(length)
    causal = (segment[:, None] == segment[None, :]) & (order[:, None] >= order[None, :])
    cum_heads = jnp.transpose(cumul, (1, 2, 0))
    differ = cum_heads[:, :, :, None] - cum_heads[:, :, None, :]
    decays = jnp.exp(jnp.where(causal, differ, -jnp.inf))
    scores = jnp.einsum('tgn,sgn->gts', c_rows, b_rows)
    mixing = decays * scores[:, None] * jnp.transpose(step_size, (1, 2, 0))[:, :, None, :]
    inside = jnp.einsum('gkts,sgkp->tgkp', mixing, seq_in, precision=HIGHEST)
    entry = jnp.exp(cumul) * reach[:, None, None]
    from_carry = entry[..., None] * jnp.einsum('tgn,gkpn->tgkp', c_rows, carried, precision=HIGHEST)
    mixer = inside + from_carry + skip_heads[..., None] * seq_in
    same_last = (segment == segment[-1]).astype(jnp.float32)
    tail = jnp.exp(cumul[-1] - cumul) * same_last[:, None, None] * step_size
    local_state = jnp.einsum('sgk,sgkp,sgn->gkpn', tail, seq_in, b_rows, precision=HIGHEST)
    through = reach[-1] * jnp.exp(cumul[-1])
    return (mixer, local_state, through)

def reference(ssm_input, dt_raw, b_proj, c_proj, dt_bias, decay_rate, skip_gain, doc_start, out_weight, grad_out):
    bias_heads = dt_bias.reshape(GROUPS, HEADS_DEV)
    rate_heads = decay_rate.reshape(GROUPS, HEADS_DEV)
    skip_heads = skip_gain.reshape(GROUPS, HEADS_DEV)
    starts = doc_start.reshape(N_CTX, TOK_DEV)
    block_fn = jax.checkpoint(block_ssd)

    def forward(seq_all, step_all, b_all, c_all):
        seq_blocks = seq_all.reshape(N_CTX, TOK_DEV, GROUPS, HEADS_DEV, HEAD_DIM)
        step_blocks = step_all.reshape(N_CTX, TOK_DEV, GROUPS, HEADS_DEV)
        b_blocks = b_all.reshape(N_CTX, TOK_DEV, GROUPS, STATE)
        c_blocks = c_all.reshape(N_CTX, TOK_DEV, GROUPS, STATE)

        def advance(carried, pieces):
            mixer, local_state, through = block_fn(pieces[0], pieces[1], pieces[2], pieces[3], carried, pieces[4], bias_heads, rate_heads, skip_heads)
            return (through[..., None, None] * carried + local_state, mixer)
        start_state = jnp.zeros((GROUPS, HEADS_DEV, HEAD_DIM, STATE), jnp.float32)
        _, mixers = lax.scan(advance, start_state, (seq_blocks, step_blocks, b_blocks, c_blocks, starts))
        return mixers.reshape(TOKENS, INNER)
    mixer_all, pullback = jax.vjp(forward, ssm_input.astype(jnp.float32), dt_raw, b_proj.astype(jnp.float32), c_proj.astype(jnp.float32))
    mixer_bf = mixer_all.astype(jnp.bfloat16)
    panels = jnp.transpose(mixer_bf.reshape(TOKENS, GROUPS, HEADS_DEV * HEAD_DIM), (1, 0, 2))
    weight_panels = out_weight.reshape(GROUPS, HEADS_DEV * HEAD_DIM, WIDTH)

    def add_panel(total, pair):
        partial_sum = jnp.dot(pair[0], pair[1], preferred_element_type=jnp.float32).astype(jnp.bfloat16)
        partial_sum = lax.optimization_barrier(partial_sum)
        return (total + partial_sum.astype(jnp.float32), None)
    out_sum, _ = lax.scan(add_panel, jnp.zeros((TOKENS, WIDTH), jnp.float32), (panels, weight_panels))
    layer_out = out_sum.astype(jnp.bfloat16)
    grad_mix = lax.dot_general(grad_out, out_weight, (((1,), (1,)), ((), ())), preferred_element_type=jnp.float32).astype(jnp.bfloat16)
    grad_seq, grad_step, grad_brows, grad_crows = pullback(grad_mix.astype(jnp.float32))
    weight_grad = lax.dot_general(grad_out, mixer_bf, (((0,), (0,)), ((), ())), preferred_element_type=jnp.float32).astype(jnp.bfloat16)
    return (layer_out, grad_seq.astype(jnp.bfloat16), grad_step, grad_brows.astype(jnp.bfloat16), grad_crows.astype(jnp.bfloat16), weight_grad)
```

```python
import functools
import jax
import jax.numpy as jnp
from jax import lax
from jax.experimental import pallas as pl
from jax.experimental.pallas import tpu as pltpu
from jax.sharding import PartitionSpec as P

F32 = jnp.float32
BF16 = jnp.bfloat16
HIGHEST = lax.Precision.HIGHEST
MASKED = -1e30


def dot(a, b, dims, precision=None):
    return lax.dot_general(
        a, b, ((dims[:1], dims[1:]), ((), ())), precision=precision, preferred_element_type=F32
    )


def spread(cols, pair, width):
    lane = lax.broadcasted_iota(jnp.int32, (1, width), 1)
    first, second = cols[:, 2 * pair : 2 * pair + 1], cols[:, 2 * pair + 1 : 2 * pair + 2]
    return jnp.where(lane < width // 2, first, second)


def triangle(rows):
    down = lax.broadcasted_iota(jnp.int32, (rows, rows), 0)
    across = lax.broadcasted_iota(jnp.int32, (rows, rows), 1)
    return down >= across


def prepare_kernel(
    x_ref, dt_ref, b_ref, bias_ref, rate_ref, docc_ref, docr_ref,
    step_ref, stept_ref, cum_ref, cumt_ref, entry_ref, tail_ref, through_ref, mask_ref, state_ref,
):
    rows, heads = dt_ref.shape
    pair_width = 2 * (x_ref.shape[1] // heads)
    tri = triangle(rows)
    step = jax.nn.softplus(dt_ref[...] + bias_ref[...])
    cum = dot(tri.astype(F32), -step * rate_ref[...], (1, 0), HIGHEST)
    seg_col = jnp.sum(jnp.where(tri, docr_ref[...], 0.0), axis=1, keepdims=True)
    down = lax.broadcasted_iota(jnp.int32, (rows, rows), 0)
    across = lax.broadcasted_iota(jnp.int32, (rows, rows), 1)
    seg_row = jnp.sum(jnp.where(down <= across, docc_ref[...], 0.0), axis=0, keepdims=True)
    total = jnp.sum(docr_ref[...], axis=1, keepdims=True)
    reach = (seg_col == 0.0).astype(F32)
    last = cum[rows - 1 : rows, :]
    entry_ref[...] = jnp.exp(cum) * reach
    tail = jnp.exp(last - cum) * (seg_col == total).astype(F32) * step
    tail_ref[...] = tail
    through_ref[...] = jnp.exp(last) * (total == 0.0).astype(F32)
    step_ref[...] = step
    stept_ref[...] = jnp.transpose(step)
    cum_ref[...] = cum
    cumt_ref[...] = jnp.transpose(cum)
    mask_ref[...] = jnp.where(tri & (seg_col == seg_row), 0.0, MASKED)
    b = b_ref[...]
    for pair in range(heads // 2):
        at = slice(pair * pair_width, (pair + 1) * pair_width)
        scaled = (spread(tail, pair, pair_width) * x_ref[:, at].astype(F32)).astype(BF16)
        state_ref[at, :] = dot(scaled, b, (0, 0)).astype(BF16)


def forward_kernel(
    x_ref, b_ref, c_ref, stept_ref, cum_ref, cumt_ref, entry_ref, skip_ref, mask_ref, carried_ref,
    out_ref,
):
    rows, heads = cum_ref.shape
    width = 2 * (x_ref.shape[1] // heads)
    lane = lax.broadcasted_iota(jnp.int32, (1, width), 1)
    c = c_ref[...]
    scores = dot(c, b_ref[...], (1, 1))
    mask = mask_ref[...]
    for pair in range(heads // 2):
        at = slice(pair * width, (pair + 1) * width)
        x = x_ref[:, at]
        parts = []
        for k in (2 * pair, 2 * pair + 1):
            decay = jnp.exp(cum_ref[:, k : k + 1] - cumt_ref[k : k + 1, :] + mask)
            mixing = decay * stept_ref[k : k + 1, :] * scores
            parts.append(dot(mixing.astype(BF16), x, (1, 0)))
        inside = jnp.where(lane < width // 2, parts[0], parts[1])
        carry = spread(entry_ref, pair, width) * dot(c, carried_ref[at, :], (1, 1))
        out_ref[:, at] = (inside + carry + spread(skip_ref, pair, width) * x.astype(F32)).astype(BF16)


def backward_kernel(
    x_ref, b_ref, c_ref, g_ref, dt_ref, bias_ref, rate_ref, step_ref, stept_ref, cum_ref, cumt_ref,
    entry_ref, tail_ref, through_ref, skip_ref, mask_ref, carried_ref, next_ref,
    dx_ref, ddt_ref, db_ref, dc_ref,
):
    rows, heads = cum_ref.shape
    width = 2 * (x_ref.shape[1] // heads)
    half = width // 2
    lane = lax.broadcasted_iota(jnp.int32, (1, width), 1)
    head_lane = lax.broadcasted_iota(jnp.int32, (1, heads), 1)
    head_row = lax.broadcasted_iota(jnp.int32, (heads, 1), 0)
    c, b = c_ref[...], b_ref[...]
    scores = dot(c, b, (1, 1))
    mask = mask_ref[...]
    dscores = jnp.zeros((rows, rows), F32)
    db = jnp.zeros(b.shape, F32)
    dc = jnp.zeros(c.shape, F32)
    row_sums = jnp.zeros((rows, heads), F32)
    col_sums = jnp.zeros((heads, rows), F32)
    dentry = jnp.zeros((rows, heads), F32)
    dtail = jnp.zeros((rows, heads), F32)
    dthrough = jnp.zeros((1, heads), F32)
    for pair in range(heads // 2):
        at = slice(pair * width, (pair + 1) * width)
        x, g = x_ref[:, at], g_ref[:, at]
        x32, g32 = x.astype(F32), g.astype(F32)
        carried, later = carried_ref[at, :], next_ref[at, :]
        from_carry = dot(c, carried, (1, 1)) * g32
        from_next = dot(b, later, (1, 1))
        tail_pair = spread(tail_ref, pair, width)
        scaled_g = (spread(entry_ref, pair, width) * g32).astype(BF16)
        scaled_x = (tail_pair * x32).astype(BF16)
        dc = dc + dot(scaled_g, carried, (1, 0))
        db = db + dot(scaled_x, later, (1, 0))
        both = carried.astype(F32) * later.astype(F32)
        tail_part = from_next * x32
        parts = []
        for j, k in enumerate((2 * pair, 2 * pair + 1)):
            mine = (lane < half) if j == 0 else (lane >= half)
            decay = jnp.exp(cum_ref[:, k : k + 1] - cumt_ref[k : k + 1, :] + mask)
            stepped = decay * stept_ref[k : k + 1, :]
            mixing = stepped * scores
            dmixing = dot(jnp.where(mine, g, jnp.zeros_like(g)), x, (1, 1))
            parts.append(dot(mixing.astype(BF16), g, (0, 0)))
            dscores = dscores + dmixing * stepped
            product = dmixing * mixing
            row_sums = jnp.where(
                head_lane == k, jnp.sum(product, axis=1, keepdims=True), row_sums
            )
            col_sums = jnp.where(
                head_row == k, jnp.sum(product, axis=0, keepdims=True), col_sums
            )
            dentry = jnp.where(
                head_lane == k,
                jnp.sum(jnp.where(mine, from_carry, 0.0), axis=1, keepdims=True),
                dentry,
            )
            dtail = jnp.where(
                head_lane == k,
                jnp.sum(jnp.where(mine, tail_part, 0.0), axis=1, keepdims=True),
                dtail,
            )
            own = jnp.sum(both[j * half : (j + 1) * half, :], axis=0, keepdims=True)
            dthrough = jnp.where(
                head_lane == k, jnp.sum(own, axis=1, keepdims=True), dthrough
            )
        inside = jnp.where(lane < half, parts[0], parts[1])
        skip = spread(skip_ref, pair, width)
        dx_ref[:, at] = (inside + tail_pair * from_next + skip * g32).astype(BF16)
    ds = dscores.astype(BF16)
    dc_ref[...] = (dc + dot(ds, b, (1, 0))).astype(BF16)
    db_ref[...] = (db + dot(ds, c, (0, 0))).astype(BF16)
    step = step_ref[...]
    tail_flow = dtail * tail_ref[...]
    col = jnp.transpose(col_sums)
    dcum = row_sums - col + dentry * entry_ref[...] - tail_flow
    at_last = jnp.sum(tail_flow, axis=0, keepdims=True) + dthrough * through_ref[...]
    down = lax.broadcasted_iota(jnp.int32, (rows, rows), 0)
    across = lax.broadcasted_iota(jnp.int32, (rows, rows), 1)
    upper = (down <= across).astype(F32)
    dlog = dot(upper, dcum, (1, 0), HIGHEST) + at_last
    dstep = (col + tail_flow) / step - dlog * rate_ref[...]
    ddt_ref[...] = dstep * jax.nn.sigmoid(dt_ref[...] + bias_ref[...])


def call(kernel, outs, *args, name):
    return pl.pallas_call(
        kernel,
        out_shape=[jax.ShapeDtypeStruct(shape, kind) for shape, kind in outs],
        compiler_params=pltpu.CompilerParams(vmem_limit_bytes=48 * 1024 * 1024),
        name=name,
    )(*args)


def swap(value):
    return lax.all_to_all(value, "ctx", 0, 0, tiled=False)


def weight_kernel(count, *refs):
    grads, mixers, out_ref = refs[:count], refs[count : 2 * count], refs[2 * count]
    total = dot(grads[0][...], mixers[0][...], (0, 0))
    for k in range(1, count):
        total = total + dot(grads[k][...], mixers[k][...], (0, 0))
    out_ref[...] = total.astype(BF16)


def shards(
    ssm_input, dt_raw, b_proj, c_proj, dt_bias, decay_rate, skip_gain, doc_start, out_weight, grad_out
):
    rows, inner = ssm_input.shape
    heads = dt_raw.shape[1]
    state = b_proj.shape[2]
    n = lax.axis_size("ctx")
    me = lax.axis_index("ctx")
    grad_full = lax.all_gather(grad_out, "tp", axis=0, tiled=True)

    b = b_proj.reshape(rows, state)
    c = c_proj.reshape(rows, state)
    bias, rate, skip = (v.reshape(1, heads) for v in (dt_bias, decay_rate, skip_gain))
    doc = doc_start.astype(F32)
    th = ((rows, heads), F32)
    ht = ((heads, rows), F32)
    step, stept, cum, cumt, entry, tail, through, mask, local_state = call(
        prepare_kernel,
        [th, ht, th, ht, th, th, ((1, heads), F32), ((rows, rows), F32), ((inner, state), BF16)],
        ssm_input, dt_raw, b, bias, rate, doc.reshape(rows, 1), doc.reshape(1, rows),
        name="prepare",
    )

    share = inner // n
    own_heads = heads // n
    spare = jnp.broadcast_to(
        through.astype(BF16).reshape(n, own_heads, 1), (n, own_heads, 16 // own_heads * state)
    ).reshape(n, 16, state)
    arrived = swap(jnp.concatenate([local_state.reshape(n, share, state), spare], axis=1))
    locals_ = arrived[:, :share].astype(F32)
    throughs = arrived[:, share :: 16 // own_heads, :1].astype(F32)
    factors = jnp.repeat(throughs, share // own_heads, axis=1)
    before = jnp.zeros((share, state), F32)
    befores = []
    for k in range(n):
        befores.append(before.astype(BF16))
        before = factors[k] * before + locals_[k]
    carried = swap(jnp.stack(befores)).reshape(inner, state)

    (mixer_bf,) = call(
        forward_kernel, [((rows, inner), BF16)],
        ssm_input, b, c, stept, cum, cumt, entry, skip, mask, carried, name="forward",
    )
    mixers = [mixer_bf] + [
        lax.ppermute(mixer_bf, "ctx", [(s, s ^ d) for s in range(n)]) for d in range(1, n)
    ]
    layer_out = lax.psum_scatter(
        jnp.dot(mixer_bf, out_weight, preferred_element_type=F32).astype(BF16),
        "tp", scatter_dimension=0, tiled=True,
    )

    grad_mix = dot(grad_full, out_weight, (1, 1)).astype(BF16)
    columns = grad_full.shape[1] // n
    grads = []
    for d in range(n):
        piece = lax.dynamic_slice(grad_full, (0, (me ^ d) * columns), (rows, columns))
        grads.append(piece if d == 0 else lax.ppermute(piece, "ctx", [(s, s ^ d) for s in range(n)]))

    scaled = (
        grad_mix.astype(F32).reshape(rows, heads, -1) * entry[:, :, None]
    ).astype(BF16).reshape(rows, inner)
    local_grad = dot(scaled, c, (0, 0)).astype(BF16)
    locals_ = swap(local_grad.reshape(n, share, state)).astype(F32)
    after = jnp.zeros((share, state), F32)
    afters = [None] * n
    for k in reversed(range(n)):
        afters[k] = after.astype(BF16)
        after = factors[k] * after + locals_[k]
    grad_next = swap(jnp.stack(afters)).reshape(inner, state)

    dx, ddt, db, dc = call(
        backward_kernel,
        [((rows, inner), BF16), th, ((rows, state), BF16), ((rows, state), BF16)],
        ssm_input, b, c, grad_mix, dt_raw, bias, rate, step, stept, cum, cumt,
        entry, tail, through, skip, mask, carried, grad_next, name="backward",
    )
    tile = 256
    weight_grad = pl.pallas_call(
        functools.partial(weight_kernel, n),
        grid=(columns // tile,),
        in_specs=[pl.BlockSpec((rows, tile), lambda i: (0, i))] * n
        + [pl.BlockSpec((rows, inner), lambda i: (0, 0))] * n,
        out_specs=pl.BlockSpec((tile, inner), lambda i: (i, 0)),
        out_shape=jax.ShapeDtypeStruct((columns, inner), BF16),
        compiler_params=pltpu.CompilerParams(vmem_limit_bytes=48 * 1024 * 1024),
        name="weight_grad",
    )(*grads, *mixers)
    return (
        layer_out, dx, ddt, db.reshape(rows, 1, state), dc.reshape(rows, 1, state), weight_grad,
    )


def solution(mesh):
    in_specs = (
        P("ctx", "tp"), P("ctx", "tp"), P("ctx", "tp", None), P("ctx", "tp", None),
        P("tp"), P("tp"), P("tp"), P("ctx"), P("tp", None), P(("ctx", "tp"), None),
    )
    out_specs = (
        P(("ctx", "tp"), None), P("ctx", "tp"), P("ctx", "tp"),
        P("ctx", "tp", None), P("ctx", "tp", None), P("ctx", "tp"),
    )
    return jax.shard_map(shards, mesh=mesh, in_specs=in_specs, out_specs=out_specs, check_vma=False)
```

```python
import jax
import jax.numpy as jnp
from jax import lax
from jax.experimental import pallas as pl
from jax.experimental.pallas import tpu as pltpu
from jax.sharding import PartitionSpec as P

F32 = jnp.float32
BF16 = jnp.bfloat16
HIGHEST = lax.Precision.HIGHEST
MASKED = -1e30


def dot(a, b, dims, precision=None):
    return lax.dot_general(
        a, b, ((dims[:1], dims[1:]), ((), ())), precision=precision, preferred_element_type=F32
    )


def column(cols, k):
    lane = lax.broadcasted_iota(jnp.int32, (1, cols.shape[1]), 1)
    return jnp.sum(jnp.where(lane == k, cols, 0.0), axis=1, keepdims=True)


def spread(cols, pair, width):
    lane = lax.broadcasted_iota(jnp.int32, (1, width), 1)
    return jnp.where(lane < width // 2, column(cols, 2 * pair), column(cols, 2 * pair + 1))


def triangle(rows):
    down = lax.broadcasted_iota(jnp.int32, (rows, rows), 0)
    across = lax.broadcasted_iota(jnp.int32, (rows, rows), 1)
    return down >= across


MESH = pl.DeviceIdType.MESH


def mixer_kernel(
    x_ref, dt_ref, b_ref, c_ref, bias_ref, rate_ref, skip_ref, docc_ref, docr_ref, grad_ref, w_hbm,
    layer_ref, dx_ref, ddt_ref, db_ref, dc_ref, wgrad_ref,
    w_ref, full_ref, part_ref, hop_ref, mix_ref, cols_ref,
    pay_ref, arr_ref, back_ref, carried_ref, pay2_ref, arr2_ref, back2_ref, next_ref,
    step_ref, stept_ref, cum_ref, cumt_ref, entry_ref, tail_ref, mask_ref, scores_ref,
    gmix_ref, gacc_ref, acc_ref, sums_ref, colsum_ref, dthrough_ref,
    w_sem, ex_send, ex_recv, mix_send, mix_recv, col_send, col_recv,
    ag_send, ag_recv, hop_send, hop_recv,
):
    n, nz = lax.axis_size("ctx"), lax.axis_size("tp")
    i, me = lax.axis_index("ctx"), lax.axis_index("tp")
    rows, heads = dt_ref.shape
    width = 2 * (x_ref.shape[1] // heads)
    half = width // 2
    own = heads // n
    pairs = heads // 2
    block, model = grad_ref.shape
    columns = model // n
    lane = lax.broadcasted_iota(jnp.int32, (1, width), 1)
    head_lane = lax.broadcasted_iota(jnp.int32, (1, heads), 1)
    down = lax.broadcasted_iota(jnp.int32, (rows, rows), 0)
    across = lax.broadcasted_iota(jnp.int32, (rows, rows), 1)

    def remote(src, dst, send, recv, **where):
        return pltpu.make_async_remote_copy(
            src_ref=src, dst_ref=dst, send_sem=send, recv_sem=recv, device_id=where,
            device_id_type=MESH,
        )

    def peer(d):
        return lax.rem(i + d, n)

    barrier = pltpu.get_barrier_semaphore()
    for d in range(1, n):
        pl.semaphore_signal(barrier, inc=1, device_id={"ctx": peer(d)}, device_id_type=MESH)
    for d in range(1, nz):
        pl.semaphore_signal(
            barrier, inc=1, device_id={"tp": lax.rem(me + d, nz)}, device_id_type=MESH
        )
    pl.semaphore_wait(barrier, n + nz - 2)

    def gather_copy(side, b, src):
        to = me + 1 if side == 0 else me - 1
        return remote(src, full_ref.at[b], ag_send.at[side, b], ag_recv.at[b], tp=to)

    @pl.when(me < nz - 1)
    def _():
        gather_copy(0, me, grad_ref).start()

    @pl.when(me > 0)
    def _():
        gather_copy(1, me, grad_ref).start()

    load = pltpu.make_async_copy(w_hbm, w_ref, w_sem)
    load.start()
    full_ref[pl.ds(me, 1)] = grad_ref[...][None]

    def col_copy(b, d):
        at = pl.multiple_of(peer(d) * columns, columns)
        return remote(
            full_ref.at[b, :, pl.ds(at, columns)], cols_ref.at[d, b],
            col_send.at[b, d], col_recv.at[b, d], ctx=peer(d),
        )

    def send_cols(b):
        for d in range(1, n):
            col_copy(b, d).start()

    def gather_step(r):
        left, right = me - 1 - r, me + 1 + r

        @pl.when(left >= 0)
        def _():
            gather_copy(0, left, full_ref.at[left]).wait_recv()

            @pl.when(me < nz - 1)
            def _():
                gather_copy(0, left, full_ref.at[left]).start()

            send_cols(left)

        @pl.when(right <= nz - 1)
        def _():
            gather_copy(1, right, full_ref.at[right]).wait_recv()

            @pl.when(me > 0)
            def _():
                gather_copy(1, right, full_ref.at[right]).start()

            send_cols(right)

    def hop_copy(side, h, b):
        to = me + 1 if side == 0 else me - 1
        return remote(
            part_ref.at[b], hop_ref.at[side, h], hop_send.at[side, h], hop_recv.at[side, h], tp=to
        )

    def hop_block(side, h):
        return nz - 1 - h + me if side == 0 else h - (nz - 1 - me)

    def hop(h):
        for side in range(2):
            b = hop_block(side, h)
            place = me if side == 0 else nz - 1 - me

            @pl.when(place <= h)
            def _():
                if h > 0:

                    @pl.when(place > 0)
                    def _():
                        hop_copy(side, h - 1, b).wait_recv()
                        total = part_ref[pl.ds(b, 1)].astype(F32)
                        total = total + hop_ref[side, h - 1][None].astype(F32)
                        part_ref[pl.ds(b, 1)] = total.astype(BF16)

                hop_copy(side, h, b).start()

    def exchange(which, src, dst):
        copies = []
        for d in range(1, n):
            copy = remote(src(peer(d)), dst, ex_send.at[which, d], ex_recv.at[which, d], ctx=peer(d))
            copy.start()
            copies.append(copy)
        return copies

    def arrived(copies):
        for copy in copies:
            copy.wait_recv()

    tri = down >= across
    step = jax.nn.softplus(dt_ref[...] + bias_ref[...])
    cum = dot(tri.astype(F32), -step * rate_ref[...], (1, 0), HIGHEST)
    seg_col = jnp.sum(jnp.where(tri, docr_ref[...], 0.0), axis=1, keepdims=True)
    seg_row = jnp.sum(jnp.where(down <= across, docc_ref[...], 0.0), axis=0, keepdims=True)
    total_docs = jnp.sum(docr_ref[...], axis=1, keepdims=True)
    last = cum[rows - 1 : rows, :]
    through = jnp.exp(last) * (total_docs == 0.0).astype(F32)
    entry_ref[...] = jnp.exp(cum) * (seg_col == 0.0).astype(F32)
    tail_ref[...] = jnp.exp(last - cum) * (seg_col == total_docs).astype(F32) * step
    step_ref[...] = step
    stept_ref[...] = jnp.transpose(step)
    cum_ref[...] = cum
    cumt_ref[...] = jnp.transpose(cum)
    mask_ref[...] = jnp.where(tri & (seg_col == seg_row), 0.0, MASKED)
    scores_ref[...] = dot(c_ref[...], b_ref[...], (1, 1))

    def lanes(pair):
        return pl.ds(pl.multiple_of(pair * width, width), width)

    @pl.loop(0, pairs)
    def _(pair):
        x = x_ref[:, lanes(pair)].astype(F32)
        scaled = (spread(tail_ref[...], pair, width) * x).astype(BF16)
        state = dot(scaled, b_ref[...], (0, 0)).astype(BF16)
        for j in range(2):
            pay_ref[2 * pair + j, :half] = state[j * half : (j + 1) * half]
            factor = column(through, 2 * pair + j)
            pay_ref[2 * pair + j, half:] = jnp.broadcast_to(factor, (16, state.shape[1])).astype(BF16)

    def share(ref):
        return lambda to: ref.at[pl.ds(to * own, own)]

    moved = exchange(0, share(pay_ref), arr_ref.at[i])
    arr_ref[pl.ds(i, 1)] = pay_ref[pl.ds(i * own, own)][None]
    send_cols(me)
    arrived(moved)

    def factor(k, j):
        return arr_ref[k, j, half:].astype(F32)[:1]

    def scan(order, local_ref, out_ref):
        for j in range(own):
            state = jnp.zeros((half, arr_ref.shape[3]), F32)
            for k in order:
                out_ref[k, j] = state.astype(BF16)
                state = factor(k, j) * state + local_ref[k, j, :half].astype(F32)

    scan(range(n), arr_ref, back_ref)
    moved2 = exchange(1, lambda to: back_ref.at[to], carried_ref.at[pl.ds(i * own, own)])
    carried_ref[pl.ds(i * own, own)] = back_ref[pl.ds(i, 1)][0]
    arrived(moved2)

    def pair_state(ref, pair):
        return ref[pl.ds(2 * pair, 2)].reshape(width, ref.shape[2])

    @pl.loop(0, pairs)
    def _(pair):
        at = lanes(pair)
        x = x_ref[:, at]
        parts = []
        for j in range(2):
            k = 2 * pair + j
            decay = jnp.exp(column(cum_ref[...], k) - cumt_ref[pl.ds(k, 1), :] + mask_ref[...])
            mixing = decay * stept_ref[pl.ds(k, 1), :] * scores_ref[...]
            parts.append(dot(mixing.astype(BF16), x, (1, 0)))
        inside = jnp.where(lane < half, parts[0], parts[1])
        carry = dot(c_ref[...], pair_state(carried_ref, pair), (1, 1))
        carry = spread(entry_ref[...], pair, width) * carry
        skip = spread(skip_ref[...], pair, width)
        mix_ref[0, :, at] = (inside + carry + skip * x.astype(F32)).astype(BF16)

    mix_copies = []
    for d in range(1, n):
        copy = remote(mix_ref.at[0], mix_ref.at[d], mix_send.at[d], mix_recv.at[d], ctx=peer(d))
        copy.start()
        mix_copies.append(copy)

    gather_step(0)
    load.wait()
    tile = 1024

    @pl.loop(0, model // tile)
    def _(t):
        at = pl.ds(pl.multiple_of(t * tile, tile), tile)
        value = dot(mix_ref[0], w_ref[:, at], (1, 0)).astype(BF16)
        part_ref[:, :, at] = value.reshape(nz, block, tile)

    hop(0)
    for r in range(1, nz - 1):
        gather_step(r)
        if r < nz - 2:
            hop(r)

    gacc_ref[...] = jnp.zeros_like(gacc_ref)

    @pl.loop(0, model // tile)
    def _(t):
        at = pl.ds(pl.multiple_of(t * tile, tile), tile)
        g = full_ref[:, :, at].reshape(rows, tile)
        gacc_ref[...] += dot(g, w_ref[:, at], (1, 1))

    gmix_ref[...] = gacc_ref[...].astype(BF16)

    @pl.loop(0, pairs)
    def _(pair):
        g = gmix_ref[:, lanes(pair)].astype(F32)
        scaled = (spread(entry_ref[...], pair, width) * g).astype(BF16)
        state = dot(scaled, c_ref[...], (0, 0)).astype(BF16)
        for j in range(2):
            pay2_ref[2 * pair + j] = state[j * half : (j + 1) * half]

    moved3 = exchange(2, share(pay2_ref), arr2_ref.at[i])
    arr2_ref[pl.ds(i, 1)] = pay2_ref[pl.ds(i * own, own)][None]
    hop(nz - 2)
    arrived(moved3)
    scan(range(n - 1, -1, -1), arr2_ref, back2_ref)
    moved4 = exchange(3, lambda to: back2_ref.at[to], next_ref.at[pl.ds(i * own, own)])
    next_ref[pl.ds(i * own, own)] = back2_ref[pl.ds(i, 1)][0]

    mine = pl.ds(pl.multiple_of(i * columns, columns), columns)
    cols_ref[0] = full_ref[:, :, mine]
    for copy in mix_copies:
        copy.wait_recv()
    for b in range(nz):
        for d in range(1, n):
            col_copy(b, d).wait_recv()
    out_tile = min(256, columns)

    @pl.loop(0, columns // out_tile)
    def _(t):
        at = pl.ds(pl.multiple_of(t * out_tile, out_tile), out_tile)
        total = jnp.zeros((out_tile, mix_ref.shape[2]), F32)
        for d in range(n):
            total = total + dot(cols_ref[d, :, :, at].reshape(rows, out_tile), mix_ref[d], (0, 0))
        wgrad_ref[at, :] = total.astype(BF16)

    arrived(moved4)

    acc_ref[...] = jnp.zeros_like(acc_ref)
    sums_ref[...] = jnp.zeros_like(sums_ref)
    dthrough_ref[...] = jnp.zeros_like(dthrough_ref)

    @pl.loop(0, pairs)
    def _(pair):
        at = lanes(pair)
        x, g = x_ref[:, at], gmix_ref[:, at]
        x32, g32 = x.astype(F32), g.astype(F32)
        carried, later = pair_state(carried_ref, pair), pair_state(next_ref, pair)
        from_carry = dot(c_ref[...], carried, (1, 1)) * g32
        from_next = dot(b_ref[...], later, (1, 1))
        tail_pair = spread(tail_ref[...], pair, width)
        scaled_g = (spread(entry_ref[...], pair, width) * g32).astype(BF16)
        scaled_x = (tail_pair * x32).astype(BF16)
        acc_ref[1] += dot(scaled_x, later, (1, 0))
        acc_ref[2] += dot(scaled_g, carried, (1, 0))
        both = carried.astype(F32) * later.astype(F32)
        tail_part = from_next * x32
        parts = []
        for j in range(2):
            k = 2 * pair + j
            side = (lane < half) if j == 0 else (lane >= half)
            here = head_lane == k
            decay = jnp.exp(column(cum_ref[...], k) - cumt_ref[pl.ds(k, 1), :] + mask_ref[...])
            stepped = decay * stept_ref[pl.ds(k, 1), :]
            mixing = stepped * scores_ref[...]
            dmixing = dot(jnp.where(side, g, jnp.zeros_like(g)), x, (1, 1))
            parts.append(dot(mixing.astype(BF16), g, (0, 0)))
            acc_ref[0] += dmixing * stepped
            product = dmixing * mixing
            colsum_ref[pl.ds(k, 1), :] = jnp.sum(product, axis=0, keepdims=True)
            for slot, value in enumerate((
                product, jnp.where(side, from_carry, 0.0), jnp.where(side, tail_part, 0.0)
            )):
                summed = jnp.sum(value, axis=1, keepdims=True)
                sums_ref[slot] += jnp.where(here, summed, 0.0)
            alone = jnp.sum(both[j * half : (j + 1) * half, :], axis=0, keepdims=True)
            alone = jnp.sum(alone, axis=1, keepdims=True)
            dthrough_ref[...] += jnp.where(here, alone, 0.0)
        inside = jnp.where(lane < half, parts[0], parts[1])
        skip = spread(skip_ref[...], pair, width)
        dx_ref[:, at] = (inside + tail_pair * from_next + skip * g32).astype(BF16)

    ds = acc_ref[0].astype(BF16)
    db_ref[...] = (acc_ref[1] + dot(ds, c_ref[...], (0, 0))).astype(BF16)
    dc_ref[...] = (acc_ref[2] + dot(ds, b_ref[...], (1, 0))).astype(BF16)
    tail_flow = sums_ref[2] * tail_ref[...]
    col = jnp.transpose(colsum_ref[...])
    dcum = sums_ref[0] - col + sums_ref[1] * entry_ref[...] - tail_flow
    at_last = jnp.sum(tail_flow, axis=0, keepdims=True) + dthrough_ref[...] * through
    upper = (down <= across).astype(F32)
    dlog = dot(upper, dcum, (1, 0), HIGHEST) + at_last
    dstep = (col + tail_flow) / step_ref[...] - dlog * rate_ref[...]
    ddt_ref[...] = dstep * jax.nn.sigmoid(dt_ref[...] + bias_ref[...])

    layer_ref[...] = part_ref[pl.ds(me, 1)][0]
    for side in range(2):
        place = me if side == 0 else nz - 1 - me

        @pl.when(place > 0)
        def _():
            hop_copy(side, nz - 2, me).wait_recv()
            total = layer_ref[...].astype(F32) + hop_ref[side, nz - 2].astype(F32)
            layer_ref[...] = total.astype(BF16)

    for copy in moved + moved2 + moved3 + moved4 + mix_copies:
        copy.wait_send()
    for b in range(nz):
        for d in range(1, n):
            col_copy(b, d).wait_send()

        @pl.when((me < nz - 1) & (me >= b))
        def _():
            gather_copy(0, b, full_ref.at[b]).wait_send()

        @pl.when((me > 0) & (me <= b))
        def _():
            gather_copy(1, b, full_ref.at[b]).wait_send()

    for h in range(nz - 1):
        for side in range(2):
            place = me if side == 0 else nz - 1 - me

            @pl.when(place <= h)
            def _():
                hop_copy(side, h, hop_block(side, h)).wait_send()


def shards(
    ssm_input, dt_raw, b_proj, c_proj, dt_bias, decay_rate, skip_gain, doc_start, out_weight, grad_out
):
    rows, inner = ssm_input.shape
    heads = dt_raw.shape[1]
    state = b_proj.shape[2]
    n, nz = lax.axis_size("ctx"), lax.axis_size("tp")
    block, model = grad_out.shape
    columns = model // n
    dim, own = inner // heads, heads // n
    doc = doc_start.astype(F32)
    th, ht = (rows, heads), (heads, rows)
    V = pltpu.VMEM
    dma = pltpu.SemaphoreType.DMA
    vmem = pl.BlockSpec(memory_space=pltpu.VMEM)
    layer_out, dx, ddt, db, dc, weight_grad = pl.pallas_call(
        mixer_kernel,
        out_shape=[
            jax.ShapeDtypeStruct(shape, kind)
            for shape, kind in (
                ((block, model), BF16), ((rows, inner), BF16), (th, F32),
                ((rows, state), BF16), ((rows, state), BF16), ((columns, inner), BF16),
            )
        ],
        in_specs=[vmem] * 10 + [pl.BlockSpec(memory_space=pl.ANY)],
        out_specs=[vmem] * 6,
        scratch_shapes=[
            V((inner, model), BF16), V((nz, block, model), BF16), V((nz, block, model), BF16),
            V((2, nz - 1, block, model), BF16), V((n, rows, inner), BF16),
            V((n, nz, block, columns), BF16),
            V((heads, dim + 16, state), BF16), V((n, own, dim + 16, state), BF16),
            V((n, own, dim, state), BF16), V((heads, dim, state), BF16),
            V((heads, dim, state), BF16), V((n, own, dim, state), BF16),
            V((n, own, dim, state), BF16), V((heads, dim, state), BF16),
            V(th, F32), V(ht, F32), V(th, F32), V(ht, F32), V(th, F32), V(th, F32),
            V((rows, rows), F32), V((rows, rows), F32),
            V((rows, inner), BF16), V((rows, inner), F32), V((3, rows, state), F32),
            V((3,) + th, F32), V(ht, F32), V((1, heads), F32),
            dma, dma((4, n)), dma((4, n)), dma((n,)), dma((n,)), dma((nz, n)), dma((nz, n)),
            dma((2, nz)), dma((nz,)), dma((2, nz)), dma((2, nz)),
        ],
        compiler_params=pltpu.CompilerParams(
            collective_id=0, has_side_effects=True, vmem_limit_bytes=60 * 1024 * 1024
        ),
        name="mixer",
    )(
        ssm_input, dt_raw, b_proj.reshape(rows, state), c_proj.reshape(rows, state),
        dt_bias.reshape(1, heads), decay_rate.reshape(1, heads), skip_gain.reshape(1, heads),
        doc.reshape(rows, 1), doc.reshape(1, rows), grad_out, out_weight,
    )
    return (
        layer_out, dx, ddt, db.reshape(rows, 1, state), dc.reshape(rows, 1, state), weight_grad,
    )


def solution(mesh):
    in_specs = (
        P("ctx", "tp"), P("ctx", "tp"), P("ctx", "tp", None), P("ctx", "tp", None),
        P("tp"), P("tp"), P("tp"), P("ctx"), P("tp", None), P(("ctx", "tp"), None),
    )
    out_specs = (
        P(("ctx", "tp"), None), P("ctx", "tp"), P("ctx", "tp"),
        P("ctx", "tp", None), P("ctx", "tp", None), P("ctx", "tp"),
    )
    return jax.shard_map(shards, mesh=mesh, in_specs=in_specs, out_specs=out_specs, check_vma=False)
```

```python
import jax
import jax.numpy as jnp
from jax import lax
from jax.experimental import pallas as pl
from jax.experimental.pallas import tpu as pltpu
from jax.sharding import PartitionSpec as P

F32 = jnp.float32
BF16 = jnp.bfloat16
HIGHEST = lax.Precision.HIGHEST
MASKED = -1e30


def dot(a, b, dims, precision=None):
    return lax.dot_general(
        a, b, ((dims[:1], dims[1:]), ((), ())), precision=precision, preferred_element_type=F32
    )


def column(cols, k):
    lane = lax.broadcasted_iota(jnp.int32, (1, cols.shape[1]), 1)
    return jnp.sum(jnp.where(lane == k, cols, 0.0), axis=1, keepdims=True)


def spread(cols, pair, width):
    lane = lax.broadcasted_iota(jnp.int32, (1, width), 1)
    return jnp.where(lane < width // 2, column(cols, 2 * pair), column(cols, 2 * pair + 1))


def triangle(rows):
    down = lax.broadcasted_iota(jnp.int32, (rows, rows), 0)
    across = lax.broadcasted_iota(jnp.int32, (rows, rows), 1)
    return down >= across


MESH = pl.DeviceIdType.MESH


def mixer_kernel(
    x_ref, dt_ref, b_ref, c_ref, bias_ref, rate_ref, skip_ref, doc_ref, grad_ref, w_hbm,
    layer_ref, dx_ref, ddt_ref, db_ref, dc_ref, wgrad_ref,
    w_ref, full_ref, part_ref, hop_ref, mix_ref, cols_ref,
    pay_ref, arr_ref, back_ref, carried_ref, pay2_ref, arr2_ref, back2_ref, next_ref,
    step_ref, stept_ref, cum_ref, cumt_ref, entry_ref, tail_ref, mask_ref, scores_ref,
    gmix_ref, gacc_ref, acc_ref, sums_ref, colsum_ref, dthrough_ref,
    w_sem, ex_send, ex_recv, mix_send, mix_recv, col_send, col_recv,
    ag_send, ag_recv, hop_send, hop_recv,
):
    n, nz = lax.axis_size("ctx"), lax.axis_size("tp")
    i, me = lax.axis_index("ctx"), lax.axis_index("tp")
    heads, rows = dt_ref.shape
    width = 2 * (x_ref.shape[1] // heads)
    half = width // 2
    own = heads // n
    pairs = heads // 2
    block, model = grad_ref.shape
    columns = model // n
    lane = lax.broadcasted_iota(jnp.int32, (1, width), 1)
    head_lane = lax.broadcasted_iota(jnp.int32, (1, heads), 1)
    down = lax.broadcasted_iota(jnp.int32, (rows, rows), 0)
    across = lax.broadcasted_iota(jnp.int32, (rows, rows), 1)

    def remote(src, dst, send, recv, **where):
        return pltpu.make_async_remote_copy(
            src_ref=src, dst_ref=dst, send_sem=send, recv_sem=recv, device_id=where,
            device_id_type=MESH,
        )

    group, member = i // 2, lax.rem(i, 2)

    def peer(d):
        return 2 * lax.rem(group + d // 2, n // 2) + (member if d % 2 == 0 else 1 - member)

    barrier = pltpu.get_barrier_semaphore()
    for d in range(1, n):
        pl.semaphore_signal(barrier, inc=1, device_id={"ctx": peer(d)}, device_id_type=MESH)
    for d in range(1, nz):
        pl.semaphore_signal(
            barrier, inc=1, device_id={"tp": lax.rem(me + d, nz)}, device_id_type=MESH
        )
    pl.semaphore_wait(barrier, n + nz - 2)

    part_width = model // 2

    def piece(c):
        return pl.ds(c * part_width, part_width)

    def gather_copy(side, b, c, src=None):
        to = me + 1 if side == 0 else me - 1
        here = full_ref.at[b, :, piece(c)]
        return remote(
            here if src is None else src.at[:, piece(c)], here,
            ag_send.at[side, b, c], ag_recv.at[b, c], tp=to,
        )

    @pl.when(me < nz - 1)
    def _():
        for c in range(2):
            gather_copy(0, me, c, grad_ref).start()

    @pl.when(me > 0)
    def _():
        for c in range(2):
            gather_copy(1, me, c, grad_ref).start()

    load = pltpu.make_async_copy(w_hbm, w_ref, w_sem)
    load.start()
    full_ref[pl.ds(me, 1)] = grad_ref[...][None]

    def col_copy(b, d):
        at = pl.multiple_of(peer(d) * columns, columns)
        return remote(
            full_ref.at[b, :, pl.ds(at, columns)], cols_ref.at[d, b],
            col_send.at[b, d], col_recv.at[b, d], ctx=peer(d),
        )

    def send_cols(b):
        for d in range(1, n):
            col_copy(b, d).start()

    def gather_step(r, c):
        for side in range(2):
            b = me - 1 - r if side == 0 else me + 1 + r
            inside = b >= 0 if side == 0 else b <= nz - 1
            onward = me < nz - 1 if side == 0 else me > 0

            @pl.when(inside)
            def _():
                gather_copy(side, b, c).wait_recv()

                @pl.when(onward)
                def _():
                    gather_copy(side, b, c).start()

                if c == 1:
                    send_cols(b)

    def hop_copy(side, h, c, b):
        to = me + 1 if side == 0 else me - 1
        return remote(
            part_ref.at[b, :, piece(c)], hop_ref.at[side, h, :, piece(c)],
            hop_send.at[side, h, c], hop_recv.at[side, h, c], tp=to,
        )

    def hop_block(side, h):
        return nz - 1 - h + me if side == 0 else h - (nz - 1 - me)

    def hop(h, c):
        for side in range(2):
            b = hop_block(side, h)
            place = me if side == 0 else nz - 1 - me

            @pl.when(place <= h)
            def _():
                if h > 0:

                    @pl.when(place > 0)
                    def _():
                        hop_copy(side, h - 1, c, b).wait_recv()
                        total = part_ref[pl.ds(b, 1), :, piece(c)].astype(F32)
                        total = total + hop_ref[side, h - 1, :, piece(c)][None].astype(F32)
                        part_ref[pl.ds(b, 1), :, piece(c)] = total.astype(BF16)

                hop_copy(side, h, c, b).start()

    def exchange(which, src, dst):
        copies = []
        for d in range(1, n):
            copy = remote(src(peer(d)), dst, ex_send.at[which, d], ex_recv.at[which, d], ctx=peer(d))
            copy.start()
            copies.append(copy)
        return copies

    def arrived(copies):
        for copy in copies:
            copy.wait_recv()

    tri = down >= across
    raw = jnp.transpose(dt_ref[...]) + bias_ref[...]
    doc_row = doc_ref[...].astype(F32)
    doc_col = jnp.transpose(jnp.broadcast_to(doc_row, (8, rows)))[:, :1]
    step = jax.nn.softplus(raw)
    cum = dot(tri.astype(F32), -step * rate_ref[...], (1, 0), HIGHEST)
    seg_col = jnp.sum(jnp.where(tri, doc_row, 0.0), axis=1, keepdims=True)
    seg_row = jnp.sum(jnp.where(down <= across, doc_col, 0.0), axis=0, keepdims=True)
    total_docs = jnp.sum(doc_row, axis=1, keepdims=True)
    last = cum[rows - 1 : rows, :]
    through = jnp.exp(last) * (total_docs == 0.0).astype(F32)
    entry_ref[...] = jnp.exp(cum) * (seg_col == 0.0).astype(F32)
    tail_ref[...] = jnp.exp(last - cum) * (seg_col == total_docs).astype(F32) * step
    step_ref[...] = step
    stept_ref[...] = jnp.transpose(step)
    cum_ref[...] = cum
    cumt_ref[...] = jnp.transpose(cum)
    mask_ref[...] = jnp.where(tri & (seg_col == seg_row), 0.0, MASKED)
    scores_ref[...] = dot(c_ref[...], b_ref[...], (1, 1))

    def lanes(pair):
        return pl.ds(pl.multiple_of(pair * width, width), width)

    @pl.loop(0, pairs)
    def _(pair):
        x = x_ref[:, lanes(pair)].astype(F32)
        scaled = (spread(tail_ref[...], pair, width) * x).astype(BF16)
        state = dot(scaled, b_ref[...], (0, 0)).astype(BF16)
        for j in range(2):
            pay_ref[2 * pair + j, :half] = state[j * half : (j + 1) * half]
            factor = column(through, 2 * pair + j)
            pay_ref[2 * pair + j, half:] = jnp.broadcast_to(factor, (16, state.shape[1])).astype(BF16)

    def share(ref):
        return lambda to: ref.at[pl.ds(to * own, own)]

    moved = exchange(0, share(pay_ref), arr_ref.at[i])
    arr_ref[pl.ds(i, 1)] = pay_ref[pl.ds(i * own, own)][None]
    arrived(moved)

    def factor(k, j):
        return arr_ref[k, j, half:].astype(F32)[:1]

    def scan(order, local_ref, out_ref):
        for j in range(own):
            state = jnp.zeros((half, arr_ref.shape[3]), F32)
            for k in order:
                out_ref[k, j] = state.astype(BF16)
                state = factor(k, j) * state + local_ref[k, j, :half].astype(F32)

    scan(range(n), arr_ref, back_ref)
    moved2 = exchange(1, lambda to: back_ref.at[to], carried_ref.at[pl.ds(i * own, own)])
    carried_ref[pl.ds(i * own, own)] = back_ref[pl.ds(i, 1)][0]
    send_cols(me)
    gather_step(0, 0)
    arrived(moved2)

    def pair_state(ref, pair):
        return ref[pl.ds(2 * pair, 2)].reshape(width, ref.shape[2])

    @pl.loop(0, pairs)
    def _(pair):
        at = lanes(pair)
        x = x_ref[:, at]
        parts = []
        for j in range(2):
            k = 2 * pair + j
            decay = jnp.exp(column(cum_ref[...], k) - cumt_ref[pl.ds(k, 1), :] + mask_ref[...])
            mixing = decay * stept_ref[pl.ds(k, 1), :] * scores_ref[...]
            parts.append(dot(mixing.astype(BF16), x, (1, 0)))
        inside = jnp.where(lane < half, parts[0], parts[1])
        carry = dot(c_ref[...], pair_state(carried_ref, pair), (1, 1))
        carry = spread(entry_ref[...], pair, width) * carry
        skip = spread(skip_ref[...], pair, width)
        mix_ref[0, :, at] = (inside + carry + skip * x.astype(F32)).astype(BF16)

    def mix_copy(d):
        return remote(
            mix_ref.at[0 if d % 2 == 0 else d - 1], mix_ref.at[d], mix_send.at[d], mix_recv.at[d],
            ctx=peer(d if d % 2 == 0 else 1),
        )

    mix_copy(1).start()
    for d in range(2, n, 2):
        mix_copy(d).start()

    load.wait()
    tile = 1024

    def layer_part(c):
        @pl.loop(0, part_width // tile)
        def _(t):
            at = pl.ds(pl.multiple_of(c * part_width + t * tile, tile), tile)
            value = dot(mix_ref[0], w_ref[:, at], (1, 0)).astype(BF16)
            part_ref[:, :, at] = value.reshape(nz, block, tile)

    layer_part(0)
    hop(0, 0)
    gather_step(0, 1)
    layer_part(1)
    hop(0, 1)

    final = jnp.where(me < nz // 2, nz - 1, 0)
    gacc_ref[...] = jnp.zeros_like(gacc_ref)

    def cotangent(blocks):
        @pl.loop(0, model // tile)
        def _(t):
            at = pl.ds(pl.multiple_of(t * tile, tile), tile)
            g = jnp.concatenate([full_ref[pl.ds(b, 1), :, at][0] for b in blocks], axis=0)
            value = dot(g, w_ref[:, at], (1, 1))
            for k, b in enumerate(blocks):
                gacc_ref[pl.ds(b, 1)] += value[k * block : (k + 1) * block][None]

    for r in range(1, nz - 1):
        gather_step(r, 0)
        gather_step(r, 1)
        if r == nz - 3:
            for d in range(2, n, 2):
                mix_copy(d).wait_recv()
                mix_copy(d + 1).start()
            cotangent([lax.rem(final + k, nz) for k in range(1, nz)])
        hop(r, 0)
        if r < nz - 2:
            hop(r, 1)
    cotangent([final])
    gmix_ref[...] = gacc_ref[...].reshape(gmix_ref.shape).astype(BF16)

    @pl.loop(0, pairs)
    def _(pair):
        g = gmix_ref[:, lanes(pair)].astype(F32)
        scaled = (spread(entry_ref[...], pair, width) * g).astype(BF16)
        state = dot(scaled, c_ref[...], (0, 0)).astype(BF16)
        for j in range(2):
            pay2_ref[2 * pair + j] = state[j * half : (j + 1) * half]

    moved3 = exchange(2, share(pay2_ref), arr2_ref.at[i])
    arr2_ref[pl.ds(i, 1)] = pay2_ref[pl.ds(i * own, own)][None]
    hop(nz - 2, 1)
    arrived(moved3)
    scan(range(n - 1, -1, -1), arr2_ref, back2_ref)
    moved4 = exchange(3, lambda to: back2_ref.at[to], next_ref.at[pl.ds(i * own, own)])
    next_ref[pl.ds(i * own, own)] = back2_ref[pl.ds(i, 1)][0]

    mine = pl.ds(pl.multiple_of(i * columns, columns), columns)
    cols_ref[0] = full_ref[:, :, mine]
    for d in range(1, n, 2):
        mix_copy(d).wait_recv()
    for b in range(nz):
        for d in range(1, n):
            col_copy(b, d).wait_recv()
    out_tile = min(256, columns)

    @pl.loop(0, columns // out_tile)
    def _(t):
        at = pl.ds(pl.multiple_of(t * out_tile, out_tile), out_tile)
        total = jnp.zeros((out_tile, mix_ref.shape[2]), F32)
        for d in range(n):
            total = total + dot(cols_ref[d, :, :, at].reshape(rows, out_tile), mix_ref[d], (0, 0))
        wgrad_ref[at, :] = total.astype(BF16)

    arrived(moved4)

    acc_ref[...] = jnp.zeros_like(acc_ref)
    sums_ref[...] = jnp.zeros_like(sums_ref)
    dthrough_ref[...] = jnp.zeros_like(dthrough_ref)

    @pl.loop(0, pairs)
    def _(pair):
        at = lanes(pair)
        x, g = x_ref[:, at], gmix_ref[:, at]
        x32, g32 = x.astype(F32), g.astype(F32)
        carried, later = pair_state(carried_ref, pair), pair_state(next_ref, pair)
        from_carry = dot(c_ref[...], carried, (1, 1)) * g32
        from_next = dot(b_ref[...], later, (1, 1))
        tail_pair = spread(tail_ref[...], pair, width)
        scaled_g = (spread(entry_ref[...], pair, width) * g32).astype(BF16)
        scaled_x = (tail_pair * x32).astype(BF16)
        acc_ref[1] += dot(scaled_x, later, (1, 0))
        acc_ref[2] += dot(scaled_g, carried, (1, 0))
        both = carried.astype(F32) * later.astype(F32)
        tail_part = from_next * x32
        parts = []
        for j in range(2):
            k = 2 * pair + j
            side = (lane < half) if j == 0 else (lane >= half)
            here = head_lane == k
            decay = jnp.exp(column(cum_ref[...], k) - cumt_ref[pl.ds(k, 1), :] + mask_ref[...])
            stepped = decay * stept_ref[pl.ds(k, 1), :]
            mixing = stepped * scores_ref[...]
            dmixing = dot(jnp.where(side, g, jnp.zeros_like(g)), x, (1, 1))
            parts.append(dot(mixing.astype(BF16), g, (0, 0)))
            acc_ref[0] += dmixing * stepped
            product = dmixing * mixing
            colsum_ref[pl.ds(k, 1), :] = jnp.sum(product, axis=0, keepdims=True)
            for slot, value in enumerate((
                product, jnp.where(side, from_carry, 0.0), jnp.where(side, tail_part, 0.0)
            )):
                summed = jnp.sum(value, axis=1, keepdims=True)
                sums_ref[slot] += jnp.where(here, summed, 0.0)
            alone = jnp.sum(both[j * half : (j + 1) * half, :], axis=0, keepdims=True)
            alone = jnp.sum(alone, axis=1, keepdims=True)
            dthrough_ref[...] += jnp.where(here, alone, 0.0)
        inside = jnp.where(lane < half, parts[0], parts[1])
        skip = spread(skip_ref[...], pair, width)
        dx_ref[:, at] = (inside + tail_pair * from_next + skip * g32).astype(BF16)

    ds = acc_ref[0].astype(BF16)
    db_ref[...] = (acc_ref[1] + dot(ds, c_ref[...], (0, 0))).astype(BF16)
    dc_ref[...] = (acc_ref[2] + dot(ds, b_ref[...], (1, 0))).astype(BF16)
    tail_flow = sums_ref[2] * tail_ref[...]
    col = jnp.transpose(colsum_ref[...])
    dcum = sums_ref[0] - col + sums_ref[1] * entry_ref[...] - tail_flow
    at_last = jnp.sum(tail_flow, axis=0, keepdims=True) + dthrough_ref[...] * through
    upper = (down <= across).astype(F32)
    dlog = dot(upper, dcum, (1, 0), HIGHEST) + at_last
    dstep = (col + tail_flow) / step_ref[...] - dlog * rate_ref[...]
    ddt_ref[...] = jnp.transpose(
        dstep * jax.nn.sigmoid(jnp.transpose(dt_ref[...]) + bias_ref[...])
    )

    layer_ref[...] = part_ref[pl.ds(me, 1)][0]
    for side in range(2):
        place = me if side == 0 else nz - 1 - me

        @pl.when(place > 0)
        def _():
            for c in range(2):
                hop_copy(side, nz - 2, c, me).wait_recv()
            total = layer_ref[...].astype(F32) + hop_ref[side, nz - 2].astype(F32)
            layer_ref[...] = total.astype(BF16)

    for copy in moved + moved2 + moved3 + moved4:
        copy.wait_send()
    for d in range(1, n):
        mix_copy(d).wait_send()
    for b in range(nz):
        for d in range(1, n):
            col_copy(b, d).wait_send()

        @pl.when((me < nz - 1) & (me >= b))
        def _():
            for c in range(2):
                gather_copy(0, b, c).wait_send()

        @pl.when((me > 0) & (me <= b))
        def _():
            for c in range(2):
                gather_copy(1, b, c).wait_send()

    for h in range(nz - 1):
        for side in range(2):
            place = me if side == 0 else nz - 1 - me

            @pl.when(place <= h)
            def _():
                for c in range(2):
                    hop_copy(side, h, c, hop_block(side, h)).wait_send()


def shards(
    ssm_input, dt_raw, b_proj, c_proj, dt_bias, decay_rate, skip_gain, doc_start, out_weight, grad_out
):
    rows, inner = ssm_input.shape
    heads = dt_raw.shape[1]
    state = b_proj.shape[2]
    n, nz = lax.axis_size("ctx"), lax.axis_size("tp")
    block, model = grad_out.shape
    columns = model // n
    dim, own = inner // heads, heads // n
    th, ht = (rows, heads), (heads, rows)
    V = pltpu.VMEM
    dma = pltpu.SemaphoreType.DMA
    vmem = pl.BlockSpec(memory_space=pltpu.VMEM)
    layer_out, dx, ddt, db, dc, weight_grad = pl.pallas_call(
        mixer_kernel,
        out_shape=[
            jax.ShapeDtypeStruct(shape, kind)
            for shape, kind in (
                ((block, model), BF16), ((rows, inner), BF16), (ht, F32),
                ((rows, state), BF16), ((rows, state), BF16), ((columns, inner), BF16),
            )
        ],
        in_specs=[vmem] * 9 + [pl.BlockSpec(memory_space=pl.ANY)],
        out_specs=[vmem] * 6,
        scratch_shapes=[
            V((inner, model), BF16), V((nz, block, model), BF16), V((nz, block, model), BF16),
            V((2, nz - 1, block, model), BF16), V((n, rows, inner), BF16),
            V((n, nz, block, columns), BF16),
            V((heads, dim + 16, state), BF16), V((n, own, dim + 16, state), BF16),
            V((n, own, dim, state), BF16), V((heads, dim, state), BF16),
            V((heads, dim, state), BF16), V((n, own, dim, state), BF16),
            V((n, own, dim, state), BF16), V((heads, dim, state), BF16),
            V(th, F32), V(ht, F32), V(th, F32), V(ht, F32), V(th, F32), V(th, F32),
            V((rows, rows), F32), V((rows, rows), F32),
            V((rows, inner), BF16), V((nz, block, inner), F32), V((3, rows, state), F32),
            V((3,) + th, F32), V(ht, F32), V((1, heads), F32),
            dma, dma((4, n)), dma((4, n)), dma((n,)), dma((n,)), dma((nz, n)), dma((nz, n)),
            dma((2, nz, 2)), dma((nz, 2)), dma((2, nz, 2)), dma((2, nz, 2)),
        ],
        compiler_params=pltpu.CompilerParams(
            collective_id=0, has_side_effects=True, vmem_limit_bytes=60 * 1024 * 1024
        ),
        name="mixer",
    )(
        ssm_input, dt_raw.T, b_proj.reshape(rows, state), c_proj.reshape(rows, state),
        dt_bias.reshape(1, heads), decay_rate.reshape(1, heads), skip_gain.reshape(1, heads),
        doc_start.reshape(1, rows), grad_out, out_weight,
    )
    return (
        layer_out, dx, ddt.T, db.reshape(rows, 1, state), dc.reshape(rows, 1, state), weight_grad,
    )


def solution(mesh):
    in_specs = (
        P("ctx", "tp"), P("ctx", "tp"), P("ctx", "tp", None), P("ctx", "tp", None),
        P("tp"), P("tp"), P("tp"), P("ctx"), P("tp", None), P(("ctx", "tp"), None),
    )
    out_specs = (
        P(("ctx", "tp"), None), P("ctx", "tp"), P("ctx", "tp"),
        P("ctx", "tp", None), P("ctx", "tp", None), P("ctx", "tp"),
    )
    return jax.shard_map(shards, mesh=mesh, in_specs=in_specs, out_specs=out_specs, check_vma=False)
```

```python
import jax
import jax.numpy as jnp
from jax import lax
from jax.experimental import pallas as pl
from jax.experimental.pallas import tpu as pltpu
from jax.sharding import PartitionSpec as P

F32 = jnp.float32
BF16 = jnp.bfloat16
HIGHEST = lax.Precision.HIGHEST
MASKED = -1e30


def dot(a, b, dims, precision=None):
    return lax.dot_general(
        a, b, ((dims[:1], dims[1:]), ((), ())), precision=precision, preferred_element_type=F32
    )


def column(cols, k):
    lane = lax.broadcasted_iota(jnp.int32, (1, cols.shape[1]), 1)
    return jnp.sum(jnp.where(lane == k, cols, 0.0), axis=1, keepdims=True)


def spread(cols, pair, width):
    lane = lax.broadcasted_iota(jnp.int32, (1, width), 1)
    return jnp.where(lane < width // 2, column(cols, 2 * pair), column(cols, 2 * pair + 1))


def triangle(rows):
    down = lax.broadcasted_iota(jnp.int32, (rows, rows), 0)
    across = lax.broadcasted_iota(jnp.int32, (rows, rows), 1)
    return down >= across


MESH = pl.DeviceIdType.MESH


def mixer_kernel(
    x_ref, dt_ref, b_ref, c_ref, bias_ref, rate_ref, skip_ref, doc_ref, grad_ref, w_hbm,
    layer_ref, dx_ref, ddt_ref, db_ref, dc_ref, wgrad_ref,
    w_ref, full_ref, part_ref, hop_ref, mix_ref, cols_ref,
    pay_ref, arr_ref, back_ref, carried_ref, pay2_ref, arr2_ref, back2_ref, next_ref,
    step_ref, stept_ref, cum_ref, cumt_ref, entry_ref, tail_ref, mask_ref, scores_ref,
    gmix_ref, gacc_ref, wacc_ref, dxacc_ref, acc_ref, sums_ref, colsum_ref, dthrough_ref,
    w_sem, ex_send, ex_recv, mix_send, mix_recv, col_send, col_recv,
    ag_send, ag_recv, hop_send, hop_recv,
):
    n, nz = lax.axis_size("ctx"), lax.axis_size("tp")
    i, me = lax.axis_index("ctx"), lax.axis_index("tp")
    heads, rows = dt_ref.shape
    width = 2 * (x_ref.shape[1] // heads)
    half = width // 2
    own = heads // n
    pairs = heads // 2
    block, model = grad_ref.shape
    columns = model // n
    lane = lax.broadcasted_iota(jnp.int32, (1, width), 1)
    head_lane = lax.broadcasted_iota(jnp.int32, (1, heads), 1)
    down = lax.broadcasted_iota(jnp.int32, (rows, rows), 0)
    across = lax.broadcasted_iota(jnp.int32, (rows, rows), 1)

    def remote(src, dst, send, recv, **where):
        return pltpu.make_async_remote_copy(
            src_ref=src, dst_ref=dst, send_sem=send, recv_sem=recv, device_id=where,
            device_id_type=MESH,
        )

    group, member = i // 2, lax.rem(i, 2)

    def peer(d):
        return 2 * lax.rem(group + d // 2, n // 2) + (member if d % 2 == 0 else 1 - member)

    barrier = pltpu.get_barrier_semaphore()
    for d in range(1, n):
        pl.semaphore_signal(barrier, inc=1, device_id={"ctx": peer(d)}, device_id_type=MESH)
    for d in range(1, nz):
        pl.semaphore_signal(
            barrier, inc=1, device_id={"tp": lax.rem(me + d, nz)}, device_id_type=MESH
        )
    pl.semaphore_wait(barrier, n + nz - 2)

    part_width = model // 2

    def piece(c):
        return pl.ds(c * part_width, part_width)

    def gather_copy(side, b, c, src=None):
        to = me + 1 if side == 0 else me - 1
        here = full_ref.at[b, :, piece(c)]
        return remote(
            here if src is None else src.at[:, piece(c)], here,
            ag_send.at[side, b, c], ag_recv.at[b, c], tp=to,
        )

    @pl.when(me < nz - 1)
    def _():
        for c in range(2):
            gather_copy(0, me, c, grad_ref).start()

    @pl.when(me > 0)
    def _():
        for c in range(2):
            gather_copy(1, me, c, grad_ref).start()

    load = pltpu.make_async_copy(w_hbm, w_ref, w_sem)
    load.start()
    full_ref[pl.ds(me, 1)] = grad_ref[...][None]

    def col_copy(b, d):
        at = pl.multiple_of(peer(d) * columns, columns)
        return remote(
            full_ref.at[b, :, pl.ds(at, columns)], cols_ref.at[d, b],
            col_send.at[b, d], col_recv.at[b, d], ctx=peer(d),
        )

    def send_cols(b):
        for d in range(1, n):
            col_copy(b, d).start()

    def gather_step(r, c):
        for side in range(2):
            b = me - 1 - r if side == 0 else me + 1 + r
            inside = b >= 0 if side == 0 else b <= nz - 1
            onward = me < nz - 1 if side == 0 else me > 0

            @pl.when(inside)
            def _():
                gather_copy(side, b, c).wait_recv()

                @pl.when(onward)
                def _():
                    gather_copy(side, b, c).start()

                if c == 1:
                    send_cols(b)

    def hop_copy(side, h, c, b):
        to = me + 1 if side == 0 else me - 1
        return remote(
            part_ref.at[b, :, piece(c)], hop_ref.at[side, h, :, piece(c)],
            hop_send.at[side, h, c], hop_recv.at[side, h, c], tp=to,
        )

    def hop_block(side, h):
        return nz - 1 - h + me if side == 0 else h - (nz - 1 - me)

    def hop(h, c):
        for side in range(2):
            b = hop_block(side, h)
            place = me if side == 0 else nz - 1 - me

            @pl.when(place <= h)
            def _():
                if h > 0:

                    @pl.when(place > 0)
                    def _():
                        hop_copy(side, h - 1, c, b).wait_recv()
                        total = part_ref[pl.ds(b, 1), :, piece(c)].astype(F32)
                        total = total + hop_ref[side, h - 1, :, piece(c)][None].astype(F32)
                        part_ref[pl.ds(b, 1), :, piece(c)] = total.astype(BF16)

                hop_copy(side, h, c, b).start()

    def exchange(which, src, dst):
        copies = []
        for d in range(1, n):
            copy = remote(src(peer(d)), dst, ex_send.at[which, d], ex_recv.at[which, d], ctx=peer(d))
            copy.start()
            copies.append(copy)
        return copies

    def arrived(copies):
        for copy in copies:
            copy.wait_recv()

    tri = down >= across
    raw = jnp.transpose(dt_ref[...]) + bias_ref[...]
    doc_row = doc_ref[...].astype(F32)
    doc_col = jnp.transpose(jnp.broadcast_to(doc_row, (8, rows)))[:, :1]
    step = jax.nn.softplus(raw)
    cum = dot(tri.astype(F32), -step * rate_ref[...], (1, 0), HIGHEST)
    seg_col = jnp.sum(jnp.where(tri, doc_row, 0.0), axis=1, keepdims=True)
    seg_row = jnp.sum(jnp.where(down <= across, doc_col, 0.0), axis=0, keepdims=True)
    total_docs = jnp.sum(doc_row, axis=1, keepdims=True)
    last = cum[rows - 1 : rows, :]
    through = jnp.exp(last) * (total_docs == 0.0).astype(F32)
    entry_ref[...] = jnp.exp(cum) * (seg_col == 0.0).astype(F32)
    tail_ref[...] = jnp.exp(last - cum) * (seg_col == total_docs).astype(F32) * step
    step_ref[...] = step
    stept_ref[...] = jnp.transpose(step)
    cum_ref[...] = cum
    cumt_ref[...] = jnp.transpose(cum)
    mask_ref[...] = jnp.where(tri & (seg_col == seg_row), 0.0, MASKED)
    scores_ref[...] = dot(c_ref[...], b_ref[...], (1, 1))

    def lanes(pair):
        return pl.ds(pl.multiple_of(pair * width, width), width)

    @pl.loop(0, pairs)
    def _(pair):
        x = x_ref[:, lanes(pair)].astype(F32)
        scaled = (spread(tail_ref[...], pair, width) * x).astype(BF16)
        state = dot(scaled, b_ref[...], (0, 0)).astype(BF16)
        for j in range(2):
            pay_ref[2 * pair + j, :half] = state[j * half : (j + 1) * half]
            factor = column(through, 2 * pair + j)
            pay_ref[2 * pair + j, half:] = jnp.broadcast_to(factor, (16, state.shape[1])).astype(BF16)

    def share(ref):
        return lambda to: ref.at[pl.ds(to * own, own)]

    moved = exchange(0, share(pay_ref), arr_ref.at[i])
    arr_ref[pl.ds(i, 1)] = pay_ref[pl.ds(i * own, own)][None]
    arrived(moved)

    def factor(k, j):
        return arr_ref[k, j, half:].astype(F32)[:1]

    def scan(order, local_ref, out_ref):
        for j in range(own):
            state = jnp.zeros((half, arr_ref.shape[3]), F32)
            for k in order:
                out_ref[k, j] = state.astype(BF16)
                state = factor(k, j) * state + local_ref[k, j, :half].astype(F32)

    scan(range(n), arr_ref, back_ref)
    moved2 = exchange(1, lambda to: back_ref.at[to], carried_ref.at[pl.ds(i * own, own)])
    carried_ref[pl.ds(i * own, own)] = back_ref[pl.ds(i, 1)][0]
    send_cols(me)
    gather_step(0, 0)
    arrived(moved2)

    def pair_state(ref, pair):
        return ref[pl.ds(2 * pair, 2)].reshape(width, ref.shape[2])

    @pl.loop(0, pairs)
    def _(pair):
        at = lanes(pair)
        x = x_ref[:, at]
        parts = []
        for j in range(2):
            k = 2 * pair + j
            decay = jnp.exp(column(cum_ref[...], k) - cumt_ref[pl.ds(k, 1), :] + mask_ref[...])
            mixing = decay * stept_ref[pl.ds(k, 1), :] * scores_ref[...]
            parts.append(dot(mixing.astype(BF16), x, (1, 0)))
        inside = jnp.where(lane < half, parts[0], parts[1])
        carry = dot(c_ref[...], pair_state(carried_ref, pair), (1, 1))
        carry = spread(entry_ref[...], pair, width) * carry
        skip = spread(skip_ref[...], pair, width)
        mix_ref[0, :, at] = (inside + carry + skip * x.astype(F32)).astype(BF16)

    def mix_copy(d):
        return remote(
            mix_ref.at[0 if d % 2 == 0 else d - 1], mix_ref.at[d], mix_send.at[d], mix_recv.at[d],
            ctx=peer(d if d % 2 == 0 else 1),
        )

    mix_copy(1).start()
    for d in range(2, n, 2):
        mix_copy(d).start()

    load.wait()
    tile = 1024

    def layer_part(c):
        @pl.loop(0, part_width // tile)
        def _(t):
            at = pl.ds(pl.multiple_of(c * part_width + t * tile, tile), tile)
            value = dot(mix_ref[0], w_ref[:, at], (1, 0)).astype(BF16)
            part_ref[:, :, at] = value.reshape(nz, block, tile)

    layer_part(0)
    hop(0, 0)
    gather_step(0, 1)
    layer_part(1)
    hop(0, 1)

    inner = x_ref.shape[1]
    out_tile = min(256, columns)

    def token_rows(b):
        return pl.ds(pl.multiple_of(b * block, block), block)

    final = jnp.where(me < nz // 2, nz - 1, 0)
    gacc_ref[...] = jnp.zeros_like(gacc_ref)

    def cotangent(blocks):
        @pl.loop(0, model // tile)
        def _(t):
            at = pl.ds(pl.multiple_of(t * tile, tile), tile)
            g = jnp.concatenate([full_ref[pl.ds(b, 1), :, at][0] for b in blocks], axis=0)
            value = dot(g, w_ref[:, at], (1, 1))
            for k, b in enumerate(blocks):
                gacc_ref[pl.ds(b, 1)] += value[k * block : (k + 1) * block][None]

    for r in range(1, nz - 1):
        gather_step(r, 0)
        if r == nz - 2:
            hop(r, 0)
        gather_step(r, 1)
        if r == nz - 3:
            for d in range(2, n, 2):
                mix_copy(d).wait_recv()
                mix_copy(d + 1).start()
            cotangent([lax.rem(final + k, nz) for k in range(1, nz)])
        if r < nz - 2:
            hop(r, 0)
            hop(r, 1)
        if r == nz - 3:
            early = [lax.rem(final + k, nz) for k in range(1, nz)]
            mine = pl.ds(pl.multiple_of(i * columns, columns), columns)
            for b in early:
                cols_ref[0, pl.ds(b, 1)] = full_ref[pl.ds(b, 1), :, mine]
                for d in range(1, n):
                    col_copy(b, d).wait_recv()
            for d in range(1, n, 2):
                mix_copy(d).wait_recv()

            @pl.loop(0, columns // out_tile)
            def _(t):
                at = pl.ds(pl.multiple_of(t * out_tile, out_tile), out_tile)
                total = jnp.zeros((out_tile, inner), F32)
                for d in range(n):
                    left = [cols_ref[d, pl.ds(b, 1), :, at][0] for b in early]
                    right = [mix_ref[d, token_rows(b), :] for b in early]
                    total = total + dot(
                        jnp.concatenate(left, axis=0), jnp.concatenate(right, axis=0), (0, 0)
                    )
                wacc_ref[at, :] = total
    cotangent([final])
    gmix_ref[...] = gacc_ref[...].reshape(gmix_ref.shape).astype(BF16)

    @pl.loop(0, pairs)
    def _(pair):
        g = gmix_ref[:, lanes(pair)].astype(F32)
        scaled = (spread(entry_ref[...], pair, width) * g).astype(BF16)
        state = dot(scaled, c_ref[...], (0, 0)).astype(BF16)
        for j in range(2):
            pay2_ref[2 * pair + j] = state[j * half : (j + 1) * half]

    moved3 = exchange(2, share(pay2_ref), arr2_ref.at[i])
    arr2_ref[pl.ds(i, 1)] = pay2_ref[pl.ds(i * own, own)][None]
    hop(nz - 2, 1)

    acc_ref[...] = jnp.zeros_like(acc_ref)
    sums_ref[...] = jnp.zeros_like(sums_ref)
    dthrough_ref[...] = jnp.zeros_like(dthrough_ref)

    @pl.loop(0, pairs)
    def _(pair):
        at = lanes(pair)
        x, g = x_ref[:, at], gmix_ref[:, at]
        g32 = g.astype(F32)
        carried = pair_state(carried_ref, pair)
        from_carry = dot(c_ref[...], carried, (1, 1)) * g32
        scaled_g = (spread(entry_ref[...], pair, width) * g32).astype(BF16)
        acc_ref[2] += dot(scaled_g, carried, (1, 0))
        parts = []
        for j in range(2):
            k = 2 * pair + j
            side = (lane < half) if j == 0 else (lane >= half)
            here = head_lane == k
            decay = jnp.exp(column(cum_ref[...], k) - cumt_ref[pl.ds(k, 1), :] + mask_ref[...])
            stepped = decay * stept_ref[pl.ds(k, 1), :]
            mixing = stepped * scores_ref[...]
            dmixing = dot(jnp.where(side, g, jnp.zeros_like(g)), x, (1, 1))
            parts.append(dot(mixing.astype(BF16), g, (0, 0)))
            acc_ref[0] += dmixing * stepped
            product = dmixing * mixing
            colsum_ref[pl.ds(k, 1), :] = jnp.sum(product, axis=0, keepdims=True)
            for slot, value in enumerate((product, jnp.where(side, from_carry, 0.0))):
                summed = jnp.sum(value, axis=1, keepdims=True)
                sums_ref[slot] += jnp.where(here, summed, 0.0)
        inside = jnp.where(lane < half, parts[0], parts[1])
        dxacc_ref[:, at] = inside + spread(skip_ref[...], pair, width) * g32

    arrived(moved3)
    scan(range(n - 1, -1, -1), arr2_ref, back2_ref)
    moved4 = exchange(3, lambda to: back2_ref.at[to], next_ref.at[pl.ds(i * own, own)])
    next_ref[pl.ds(i * own, own)] = back2_ref[pl.ds(i, 1)][0]

    cols_ref[0, pl.ds(final, 1)] = full_ref[pl.ds(final, 1), :, mine]
    for d in range(1, n):
        col_copy(final, d).wait_recv()
    staged = w_ref.at[pl.ds(0, columns), pl.ds(0, inner)]

    @pl.loop(0, columns // out_tile)
    def _(t):
        at = pl.ds(pl.multiple_of(t * out_tile, out_tile), out_tile)
        left = [cols_ref[d, pl.ds(final, 1), :, at][0] for d in range(n)]
        right = [mix_ref[d, token_rows(final), :] for d in range(n)]
        total = dot(jnp.concatenate(left, axis=0), jnp.concatenate(right, axis=0), (0, 0))
        w_ref[at, pl.ds(0, inner)] = (wacc_ref[at, :] + total).astype(BF16)

    store = pltpu.make_async_copy(staged, wgrad_ref, w_sem)
    store.start()

    arrived(moved4)

    @pl.loop(0, pairs)
    def _(pair):
        at = lanes(pair)
        x32 = x_ref[:, at].astype(F32)
        carried, later = pair_state(carried_ref, pair), pair_state(next_ref, pair)
        from_next = dot(b_ref[...], later, (1, 1))
        tail_pair = spread(tail_ref[...], pair, width)
        acc_ref[1] += dot((tail_pair * x32).astype(BF16), later, (1, 0))
        both = carried.astype(F32) * later.astype(F32)
        tail_part = from_next * x32
        for j in range(2):
            side = (lane < half) if j == 0 else (lane >= half)
            here = head_lane == 2 * pair + j
            summed = jnp.sum(jnp.where(side, tail_part, 0.0), axis=1, keepdims=True)
            sums_ref[2] += jnp.where(here, summed, 0.0)
            alone = jnp.sum(both[j * half : (j + 1) * half, :], axis=0, keepdims=True)
            alone = jnp.sum(alone, axis=1, keepdims=True)
            dthrough_ref[...] += jnp.where(here, alone, 0.0)
        dx_ref[:, at] = (dxacc_ref[:, at] + tail_pair * from_next).astype(BF16)

    ds = acc_ref[0].astype(BF16)
    db_ref[...] = (acc_ref[1] + dot(ds, c_ref[...], (0, 0))).astype(BF16)
    dc_ref[...] = (acc_ref[2] + dot(ds, b_ref[...], (1, 0))).astype(BF16)
    tail_flow = sums_ref[2] * tail_ref[...]
    col = jnp.transpose(colsum_ref[...])
    dcum = sums_ref[0] - col + sums_ref[1] * entry_ref[...] - tail_flow
    at_last = jnp.sum(tail_flow, axis=0, keepdims=True) + dthrough_ref[...] * through
    upper = (down <= across).astype(F32)
    dlog = dot(upper, dcum, (1, 0), HIGHEST) + at_last
    dstep = (col + tail_flow) / step_ref[...] - dlog * rate_ref[...]
    ddt_ref[...] = jnp.transpose(
        dstep * jax.nn.sigmoid(jnp.transpose(dt_ref[...]) + bias_ref[...])
    )

    layer_ref[...] = part_ref[pl.ds(me, 1)][0]
    for side in range(2):
        place = me if side == 0 else nz - 1 - me

        @pl.when(place > 0)
        def _():
            for c in range(2):
                hop_copy(side, nz - 2, c, me).wait_recv()
            total = layer_ref[...].astype(F32) + hop_ref[side, nz - 2].astype(F32)
            layer_ref[...] = total.astype(BF16)

    store.wait()

    for copy in moved + moved2 + moved3 + moved4:
        copy.wait_send()
    for d in range(1, n):
        mix_copy(d).wait_send()
    for b in range(nz):
        for d in range(1, n):
            col_copy(b, d).wait_send()

        @pl.when((me < nz - 1) & (me >= b))
        def _():
            for c in range(2):
                gather_copy(0, b, c).wait_send()

        @pl.when((me > 0) & (me <= b))
        def _():
            for c in range(2):
                gather_copy(1, b, c).wait_send()

    for h in range(nz - 1):
        for side in range(2):
            place = me if side == 0 else nz - 1 - me

            @pl.when(place <= h)
            def _():
                for c in range(2):
                    hop_copy(side, h, c, hop_block(side, h)).wait_send()


def settle_kernel(*refs):
    sems = refs[12]
    copies = []
    for k in range(6):
        rows = refs[k].shape[0]
        cuts = 4 if rows % 64 == 0 else 1
        for cut in range(cuts):
            at = pl.ds(cut * (rows // cuts), rows // cuts)
            copies.append(pltpu.make_async_copy(refs[k].at[at], refs[6 + k].at[at], sems.at[k, cut]))
    for copy in copies:
        copy.start()
    for copy in copies:
        copy.wait()


def shards(
    ssm_input, dt_raw, b_proj, c_proj, dt_bias, decay_rate, skip_gain, doc_start, out_weight, grad_out
):
    rows, inner = ssm_input.shape
    heads = dt_raw.shape[1]
    state = b_proj.shape[2]
    n, nz = lax.axis_size("ctx"), lax.axis_size("tp")
    block, model = grad_out.shape
    columns = model // n
    dim, own = inner // heads, heads // n
    th, ht = (rows, heads), (heads, rows)
    V = pltpu.VMEM
    dma = pltpu.SemaphoreType.DMA
    vmem = pl.BlockSpec(memory_space=pltpu.VMEM)
    results = pl.pallas_call(
        mixer_kernel,
        out_shape=[
            jax.ShapeDtypeStruct(shape, kind)
            for shape, kind in (
                ((block, model), BF16), ((rows, inner), BF16), (ht, F32),
                ((rows, state), BF16), ((rows, state), BF16), ((columns, inner), BF16),
            )
        ],
        in_specs=[vmem] * 9 + [pl.BlockSpec(memory_space=pl.ANY)],
        out_specs=[vmem] * 5 + [pl.BlockSpec(memory_space=pl.ANY)],
        scratch_shapes=[
            V((inner, model), BF16), V((nz, block, model), BF16), V((nz, block, model), BF16),
            V((2, nz - 1, block, model), BF16), V((n, rows, inner), BF16),
            V((n, nz, block, columns), BF16),
            V((heads, dim + 16, state), BF16), V((n, own, dim + 16, state), BF16),
            V((n, own, dim, state), BF16), V((heads, dim, state), BF16),
            V((heads, dim, state), BF16), V((n, own, dim, state), BF16),
            V((n, own, dim, state), BF16), V((heads, dim, state), BF16),
            V(th, F32), V(ht, F32), V(th, F32), V(ht, F32), V(th, F32), V(th, F32),
            V((rows, rows), F32), V((rows, rows), F32),
            V((rows, inner), BF16), V((nz, block, inner), F32), V((columns, inner), F32), V((rows, inner), F32),
            V((3, rows, state), F32),
            V((3,) + th, F32), V(ht, F32), V((1, heads), F32),
            dma, dma((4, n)), dma((4, n)), dma((n,)), dma((n,)), dma((nz, n)), dma((nz, n)),
            dma((2, nz, 2)), dma((nz, 2)), dma((2, nz, 2)), dma((2, nz, 2)),
        ],
        compiler_params=pltpu.CompilerParams(
            collective_id=0, has_side_effects=True, vmem_limit_bytes=60 * 1024 * 1024
        ),
        name="mixer",
    )(
        ssm_input, dt_raw.T, b_proj.reshape(rows, state), c_proj.reshape(rows, state),
        dt_bias.reshape(1, heads), decay_rate.reshape(1, heads), skip_gain.reshape(1, heads),
        doc_start.reshape(1, rows), grad_out, out_weight,
    )
    anywhere = pl.BlockSpec(memory_space=pl.ANY)
    layer_out, dx, ddt, db, dc, weight_grad = pl.pallas_call(
        settle_kernel,
        out_shape=[jax.ShapeDtypeStruct(part.shape, part.dtype) for part in results],
        in_specs=[anywhere] * 6,
        out_specs=[anywhere] * 6,
        scratch_shapes=[dma((6, 4))],
        compiler_params=pltpu.CompilerParams(vmem_limit_bytes=60 * 1024 * 1024),
        name="settle",
    )(*results)
    return (
        layer_out, dx, ddt.T, db.reshape(rows, 1, state), dc.reshape(rows, 1, state), weight_grad,
    )


def solution(mesh):
    in_specs = (
        P("ctx", "tp"), P("ctx", "tp"), P("ctx", "tp", None), P("ctx", "tp", None),
        P("tp"), P("tp"), P("tp"), P("ctx"), P("tp", None), P(("ctx", "tp"), None),
    )
    out_specs = (
        P(("ctx", "tp"), None), P("ctx", "tp"), P("ctx", "tp"),
        P("ctx", "tp", None), P("ctx", "tp", None), P("ctx", "tp"),
    )
    return jax.shard_map(shards, mesh=mesh, in_specs=in_specs, out_specs=out_specs, check_vma=False)
```

```python
import jax
import jax.numpy as jnp
from jax import lax
from jax.experimental import pallas as pl
from jax.experimental.pallas import tpu as pltpu
from jax.sharding import PartitionSpec as P

F32 = jnp.float32
BF16 = jnp.bfloat16
HIGHEST = lax.Precision.HIGHEST
MASKED = -1e30


def dot(a, b, dims, precision=None):
    return lax.dot_general(
        a, b, ((dims[:1], dims[1:]), ((), ())), precision=precision, preferred_element_type=F32
    )


def column(cols, k):
    lane = lax.broadcasted_iota(jnp.int32, (1, cols.shape[1]), 1)
    return jnp.sum(jnp.where(lane == k, cols, 0.0), axis=1, keepdims=True)


def spread(cols, pair, width):
    lane = lax.broadcasted_iota(jnp.int32, (1, width), 1)
    return jnp.where(lane < width // 2, column(cols, 2 * pair), column(cols, 2 * pair + 1))


def triangle(rows):
    down = lax.broadcasted_iota(jnp.int32, (rows, rows), 0)
    across = lax.broadcasted_iota(jnp.int32, (rows, rows), 1)
    return down >= across


MESH = pl.DeviceIdType.MESH


def mixer_kernel(
    x_ref, dt_ref, b_ref, c_ref, bias_ref, rate_ref, skip_ref, doc_ref, grad_ref, w_hbm,
    layer_ref, dx_ref, ddt_ref, db_ref, dc_ref, wgrad_ref,
    w_ref, full_ref, part_ref, hop_ref, mix_ref, cols_ref,
    pay_ref, arr_ref, back_ref, carried_ref, pay2_ref, arr2_ref, back2_ref, next_ref,
    step_ref, stept_ref, cum_ref, cumt_ref, entry_ref, tail_ref, mask_ref, scores_ref,
    gmix_ref, gacc_ref, wacc_ref, dxacc_ref, acc_ref, sums_ref, colsum_ref, dthrough_ref,
    w_sem, ex_send, ex_recv, mix_send, mix_recv, col_send, col_recv,
    ag_send, ag_recv, hop_send, hop_recv,
):
    n, nz = lax.axis_size("ctx"), lax.axis_size("tp")
    i, me = lax.axis_index("ctx"), lax.axis_index("tp")
    heads, rows = dt_ref.shape
    width = 2 * (x_ref.shape[1] // heads)
    half = width // 2
    own = heads // n
    pairs = heads // 2
    block, model = grad_ref.shape
    columns = model // n
    lane = lax.broadcasted_iota(jnp.int32, (1, width), 1)
    head_lane = lax.broadcasted_iota(jnp.int32, (1, heads), 1)
    down = lax.broadcasted_iota(jnp.int32, (rows, rows), 0)
    across = lax.broadcasted_iota(jnp.int32, (rows, rows), 1)

    def remote(src, dst, send, recv, **where):
        return pltpu.make_async_remote_copy(
            src_ref=src, dst_ref=dst, send_sem=send, recv_sem=recv, device_id=where,
            device_id_type=MESH,
        )

    group, member = i // 2, lax.rem(i, 2)

    def peer(d):
        return 2 * lax.rem(group + d // 2, n // 2) + (member if d % 2 == 0 else 1 - member)

    barrier = pltpu.get_barrier_semaphore()
    for d in range(1, n):
        pl.semaphore_signal(barrier, inc=1, device_id={"ctx": peer(d)}, device_id_type=MESH)
    for d in range(1, nz):
        pl.semaphore_signal(
            barrier, inc=1, device_id={"tp": lax.rem(me + d, nz)}, device_id_type=MESH
        )
    pl.semaphore_wait(barrier, n + nz - 2)

    part_width = model // 2

    def piece(c):
        return pl.ds(c * part_width, part_width)

    part_rows = block // 2

    def row_piece(c):
        return pl.ds(c * part_rows, part_rows)

    def gather_copy(side, b, c, src=None):
        to = me + 1 if side == 0 else me - 1
        here = full_ref.at[b, row_piece(c)]
        return remote(
            here if src is None else src.at[row_piece(c)], here,
            ag_send.at[side, b, c], ag_recv.at[b, c], tp=to,
        )

    @pl.when(me < nz - 1)
    def _():
        for c in range(2):
            gather_copy(0, me, c, grad_ref).start()

    @pl.when(me > 0)
    def _():
        for c in range(2):
            gather_copy(1, me, c, grad_ref).start()

    load = pltpu.make_async_copy(w_hbm, w_ref, w_sem)
    load.start()
    full_ref[pl.ds(me, 1)] = grad_ref[...][None]

    def col_copy(b, c, d):
        at = pl.multiple_of(peer(d) * columns, columns)
        return remote(
            full_ref.at[b, row_piece(c), pl.ds(at, columns)], cols_ref.at[d, b, row_piece(c)],
            col_send.at[b, c, d], col_recv.at[b, c, d], ctx=peer(d),
        )

    def send_cols(b, c):
        for d in range(1, n):
            col_copy(b, c, d).start()

    def gather_step(r, c):
        for side in range(2):
            b = me - 1 - r if side == 0 else me + 1 + r
            inside = b >= 0 if side == 0 else b <= nz - 1
            onward = me < nz - 1 if side == 0 else me > 0

            @pl.when(inside)
            def _():
                gather_copy(side, b, c).wait_recv()

                @pl.when(onward)
                def _():
                    gather_copy(side, b, c).start()

                send_cols(b, c)

    def hop_copy(side, h, c, b):
        to = me + 1 if side == 0 else me - 1
        return remote(
            part_ref.at[b, :, piece(c)], hop_ref.at[side, h, :, piece(c)],
            hop_send.at[side, h, c], hop_recv.at[side, h, c], tp=to,
        )

    def hop_block(side, h):
        return nz - 1 - h + me if side == 0 else h - (nz - 1 - me)

    def hop(h, c):
        for side in range(2):
            b = hop_block(side, h)
            place = me if side == 0 else nz - 1 - me

            @pl.when(place <= h)
            def _():
                if h > 0:

                    @pl.when(place > 0)
                    def _():
                        hop_copy(side, h - 1, c, b).wait_recv()
                        total = part_ref[pl.ds(b, 1), :, piece(c)].astype(F32)
                        total = total + hop_ref[side, h - 1, :, piece(c)][None].astype(F32)
                        part_ref[pl.ds(b, 1), :, piece(c)] = total.astype(BF16)

                hop_copy(side, h, c, b).start()

    def exchange(which, src, dst):
        copies = []
        for d in range(1, n):
            copy = remote(src(peer(d)), dst, ex_send.at[which, d], ex_recv.at[which, d], ctx=peer(d))
            copy.start()
            copies.append(copy)
        return copies

    def arrived(copies):
        for copy in copies:
            copy.wait_recv()

    tri = down >= across
    raw = jnp.transpose(dt_ref[...]) + bias_ref[...]
    doc_row = doc_ref[...].astype(F32)
    doc_col = jnp.transpose(jnp.broadcast_to(doc_row, (8, rows)))[:, :1]
    step = jax.nn.softplus(raw)
    cum = dot(tri.astype(F32), -step * rate_ref[...], (1, 0), HIGHEST)
    seg_col = jnp.sum(jnp.where(tri, doc_row, 0.0), axis=1, keepdims=True)
    seg_row = jnp.sum(jnp.where(down <= across, doc_col, 0.0), axis=0, keepdims=True)
    total_docs = jnp.sum(doc_row, axis=1, keepdims=True)
    last = cum[rows - 1 : rows, :]
    through = jnp.exp(last) * (total_docs == 0.0).astype(F32)
    entry_ref[...] = jnp.exp(cum) * (seg_col == 0.0).astype(F32)
    tail_ref[...] = jnp.exp(last - cum) * (seg_col == total_docs).astype(F32) * step
    step_ref[...] = step
    stept_ref[...] = jnp.transpose(step)
    cum_ref[...] = cum
    cumt_ref[...] = jnp.transpose(cum)
    mask_ref[...] = jnp.where(tri & (seg_col == seg_row), 0.0, MASKED)
    scores_ref[...] = dot(c_ref[...], b_ref[...], (1, 1))

    def lanes(pair):
        return pl.ds(pl.multiple_of(pair * width, width), width)

    @pl.loop(0, pairs)
    def _(pair):
        x = x_ref[:, lanes(pair)].astype(F32)
        scaled = (spread(tail_ref[...], pair, width) * x).astype(BF16)
        state = dot(scaled, b_ref[...], (0, 0)).astype(BF16)
        for j in range(2):
            pay_ref[2 * pair + j, :half] = state[j * half : (j + 1) * half]
            factor = column(through, 2 * pair + j)
            pay_ref[2 * pair + j, half:] = jnp.broadcast_to(factor, (16, state.shape[1])).astype(BF16)

    def share(ref):
        return lambda to: ref.at[pl.ds(to * own, own)]

    moved = exchange(0, share(pay_ref), arr_ref.at[i])
    arr_ref[pl.ds(i, 1)] = pay_ref[pl.ds(i * own, own)][None]
    arrived(moved)

    def factor(k, j):
        return arr_ref[k, j, half:].astype(F32)[:1]

    def scan(order, local_ref, out_ref):
        for j in range(own):
            state = jnp.zeros((half, arr_ref.shape[3]), F32)
            for k in order:
                out_ref[k, j] = state.astype(BF16)
                state = factor(k, j) * state + local_ref[k, j, :half].astype(F32)

    scan(range(n), arr_ref, back_ref)
    moved2 = exchange(1, lambda to: back_ref.at[to], carried_ref.at[pl.ds(i * own, own)])
    carried_ref[pl.ds(i * own, own)] = back_ref[pl.ds(i, 1)][0]
    send_cols(me, 0)
    send_cols(me, 1)
    gather_step(0, 0)
    arrived(moved2)

    def pair_state(ref, pair):
        return ref[pl.ds(2 * pair, 2)].reshape(width, ref.shape[2])

    @pl.loop(0, pairs)
    def _(pair):
        at = lanes(pair)
        x = x_ref[:, at]
        parts = []
        for j in range(2):
            k = 2 * pair + j
            decay = jnp.exp(column(cum_ref[...], k) - cumt_ref[pl.ds(k, 1), :] + mask_ref[...])
            mixing = decay * stept_ref[pl.ds(k, 1), :] * scores_ref[...]
            parts.append(dot(mixing.astype(BF16), x, (1, 0)))
        inside = jnp.where(lane < half, parts[0], parts[1])
        carry = dot(c_ref[...], pair_state(carried_ref, pair), (1, 1))
        carry = spread(entry_ref[...], pair, width) * carry
        skip = spread(skip_ref[...], pair, width)
        mix_ref[0, :, at] = (inside + carry + skip * x.astype(F32)).astype(BF16)

    def mix_copy(d):
        return remote(
            mix_ref.at[0 if d % 2 == 0 else d - 1], mix_ref.at[d], mix_send.at[d], mix_recv.at[d],
            ctx=peer(d if d % 2 == 0 else 1),
        )

    mix_copy(1).start()
    for d in range(2, n, 2):
        mix_copy(d).start()

    load.wait()
    tile = 1024

    def layer_part(c):
        @pl.loop(0, part_width // tile)
        def _(t):
            at = pl.ds(pl.multiple_of(c * part_width + t * tile, tile), tile)
            value = dot(mix_ref[0], w_ref[:, at], (1, 0)).astype(BF16)
            part_ref[:, :, at] = value.reshape(nz, block, tile)

    layer_part(0)
    hop(0, 0)
    gather_step(0, 1)
    layer_part(1)
    hop(0, 1)

    inner = x_ref.shape[1]
    out_tile = min(256, columns)

    def token_rows(b):
        return pl.ds(pl.multiple_of(b * block, block), block)

    final = jnp.where(me < nz // 2, nz - 1, 0)
    gacc_ref[...] = jnp.zeros_like(gacc_ref)

    def cotangent(blocks):
        @pl.loop(0, model // tile)
        def _(t):
            at = pl.ds(pl.multiple_of(t * tile, tile), tile)
            g = jnp.concatenate([full_ref[pl.ds(b, 1), :, at][0] for b in blocks], axis=0)
            value = dot(g, w_ref[:, at], (1, 1))
            for k, b in enumerate(blocks):
                gacc_ref[pl.ds(b, 1)] += value[k * block : (k + 1) * block][None]

    for r in range(1, nz - 2):
        gather_step(r, 0)
        hop(r, 0)
        gather_step(r, 1)
        hop(r, 1)
    for d in range(2, n, 2):
        mix_copy(d).wait_recv()
        mix_copy(d + 1).start()
    early = [lax.rem(final + k, nz) for k in range(1, nz)]
    cotangent(early)
    gather_step(nz - 2, 0)
    hop(nz - 2, 0)

    mine = pl.ds(pl.multiple_of(i * columns, columns), columns)
    for b in early:
        cols_ref[0, pl.ds(b, 1)] = full_ref[pl.ds(b, 1), :, mine]
        for d in range(1, n):
            for c in range(2):
                col_copy(b, c, d).wait_recv()
    for d in range(1, n, 2):
        mix_copy(d).wait_recv()

    @pl.loop(0, columns // out_tile)
    def _(t):
        at = pl.ds(pl.multiple_of(t * out_tile, out_tile), out_tile)
        total = jnp.zeros((out_tile, inner), F32)
        for d in range(n):
            left = [cols_ref[d, pl.ds(b, 1), :, at][0] for b in early]
            right = [mix_ref[d, token_rows(b), :] for b in early]
            total = total + dot(
                jnp.concatenate(left, axis=0), jnp.concatenate(right, axis=0), (0, 0)
            )
        wacc_ref[at, :] = total
    hop(nz - 2, 1)
    gather_step(nz - 2, 1)
    cotangent([final])
    gmix_ref[...] = gacc_ref[...].reshape(gmix_ref.shape).astype(BF16)

    @pl.loop(0, pairs)
    def _(pair):
        g = gmix_ref[:, lanes(pair)].astype(F32)
        scaled = (spread(entry_ref[...], pair, width) * g).astype(BF16)
        state = dot(scaled, c_ref[...], (0, 0)).astype(BF16)
        for j in range(2):
            pay2_ref[2 * pair + j] = state[j * half : (j + 1) * half]

    moved3 = exchange(2, share(pay2_ref), arr2_ref.at[i])
    arr2_ref[pl.ds(i, 1)] = pay2_ref[pl.ds(i * own, own)][None]

    acc_ref[...] = jnp.zeros_like(acc_ref)
    sums_ref[...] = jnp.zeros_like(sums_ref)
    dthrough_ref[...] = jnp.zeros_like(dthrough_ref)

    @pl.loop(0, pairs)
    def _(pair):
        at = lanes(pair)
        x, g = x_ref[:, at], gmix_ref[:, at]
        g32 = g.astype(F32)
        carried = pair_state(carried_ref, pair)
        from_carry = dot(c_ref[...], carried, (1, 1)) * g32
        scaled_g = (spread(entry_ref[...], pair, width) * g32).astype(BF16)
        acc_ref[2] += dot(scaled_g, carried, (1, 0))
        parts = []
        for j in range(2):
            k = 2 * pair + j
            side = (lane < half) if j == 0 else (lane >= half)
            here = head_lane == k
            decay = jnp.exp(column(cum_ref[...], k) - cumt_ref[pl.ds(k, 1), :] + mask_ref[...])
            stepped = decay * stept_ref[pl.ds(k, 1), :]
            mixing = stepped * scores_ref[...]
            dmixing = dot(jnp.where(side, g, jnp.zeros_like(g)), x, (1, 1))
            parts.append(dot(mixing.astype(BF16), g, (0, 0)))
            acc_ref[0] += dmixing * stepped
            product = dmixing * mixing
            colsum_ref[pl.ds(k, 1), :] = jnp.sum(product, axis=0, keepdims=True)
            for slot, value in enumerate((product, jnp.where(side, from_carry, 0.0))):
                summed = jnp.sum(value, axis=1, keepdims=True)
                sums_ref[slot] += jnp.where(here, summed, 0.0)
        inside = jnp.where(lane < half, parts[0], parts[1])
        dxacc_ref[:, at] = inside + spread(skip_ref[...], pair, width) * g32

    arrived(moved3)
    scan(range(n - 1, -1, -1), arr2_ref, back2_ref)
    moved4 = exchange(3, lambda to: back2_ref.at[to], next_ref.at[pl.ds(i * own, own)])
    next_ref[pl.ds(i * own, own)] = back2_ref[pl.ds(i, 1)][0]

    cols_ref[0, pl.ds(final, 1)] = full_ref[pl.ds(final, 1), :, mine]
    for d in range(1, n):
        for c in range(2):
            col_copy(final, c, d).wait_recv()
    staged = w_ref.at[pl.ds(0, columns), pl.ds(0, inner)]

    @pl.loop(0, columns // out_tile)
    def _(t):
        at = pl.ds(pl.multiple_of(t * out_tile, out_tile), out_tile)
        left = [cols_ref[d, pl.ds(final, 1), :, at][0] for d in range(n)]
        right = [mix_ref[d, token_rows(final), :] for d in range(n)]
        total = dot(jnp.concatenate(left, axis=0), jnp.concatenate(right, axis=0), (0, 0))
        w_ref[at, pl.ds(0, inner)] = (wacc_ref[at, :] + total).astype(BF16)

    store = pltpu.make_async_copy(staged, wgrad_ref, w_sem)
    store.start()

    arrived(moved4)

    @pl.loop(0, pairs)
    def _(pair):
        at = lanes(pair)
        x32 = x_ref[:, at].astype(F32)
        carried, later = pair_state(carried_ref, pair), pair_state(next_ref, pair)
        from_next = dot(b_ref[...], later, (1, 1))
        tail_pair = spread(tail_ref[...], pair, width)
        acc_ref[1] += dot((tail_pair * x32).astype(BF16), later, (1, 0))
        both = carried.astype(F32) * later.astype(F32)
        tail_part = from_next * x32
        for j in range(2):
            side = (lane < half) if j == 0 else (lane >= half)
            here = head_lane == 2 * pair + j
            summed = jnp.sum(jnp.where(side, tail_part, 0.0), axis=1, keepdims=True)
            sums_ref[2] += jnp.where(here, summed, 0.0)
            alone = jnp.sum(both[j * half : (j + 1) * half, :], axis=0, keepdims=True)
            alone = jnp.sum(alone, axis=1, keepdims=True)
            dthrough_ref[...] += jnp.where(here, alone, 0.0)
        dx_ref[:, at] = (dxacc_ref[:, at] + tail_pair * from_next).astype(BF16)

    ds = acc_ref[0].astype(BF16)
    db_ref[...] = (acc_ref[1] + dot(ds, c_ref[...], (0, 0))).astype(BF16)
    dc_ref[...] = (acc_ref[2] + dot(ds, b_ref[...], (1, 0))).astype(BF16)
    tail_flow = sums_ref[2] * tail_ref[...]
    col = jnp.transpose(colsum_ref[...])
    dcum = sums_ref[0] - col + sums_ref[1] * entry_ref[...] - tail_flow
    at_last = jnp.sum(tail_flow, axis=0, keepdims=True) + dthrough_ref[...] * through
    upper = (down <= across).astype(F32)
    dlog = dot(upper, dcum, (1, 0), HIGHEST) + at_last
    dstep = (col + tail_flow) / step_ref[...] - dlog * rate_ref[...]
    ddt_ref[...] = jnp.transpose(
        dstep * jax.nn.sigmoid(jnp.transpose(dt_ref[...]) + bias_ref[...])
    )

    layer_ref[...] = part_ref[pl.ds(me, 1)][0]
    for side in range(2):
        place = me if side == 0 else nz - 1 - me

        @pl.when(place > 0)
        def _():
            for c in range(2):
                hop_copy(side, nz - 2, c, me).wait_recv()
            total = layer_ref[...].astype(F32) + hop_ref[side, nz - 2].astype(F32)
            layer_ref[...] = total.astype(BF16)

    store.wait()

    for copy in moved + moved2 + moved3 + moved4:
        copy.wait_send()
    for d in range(1, n):
        mix_copy(d).wait_send()
    for b in range(nz):
        for d in range(1, n):
            for c in range(2):
                col_copy(b, c, d).wait_send()

        @pl.when((me < nz - 1) & (me >= b))
        def _():
            for c in range(2):
                gather_copy(0, b, c).wait_send()

        @pl.when((me > 0) & (me <= b))
        def _():
            for c in range(2):
                gather_copy(1, b, c).wait_send()

    for h in range(nz - 1):
        for side in range(2):
            place = me if side == 0 else nz - 1 - me

            @pl.when(place <= h)
            def _():
                for c in range(2):
                    hop_copy(side, h, c, hop_block(side, h)).wait_send()


def settle_kernel(*refs):
    sems = refs[12]
    copies = []
    for k in range(6):
        rows = refs[k].shape[0]
        cuts = 4 if rows % 64 == 0 else 1
        for cut in range(cuts):
            at = pl.ds(cut * (rows // cuts), rows // cuts)
            copies.append(pltpu.make_async_copy(refs[k].at[at], refs[6 + k].at[at], sems.at[k, cut]))
    for copy in copies:
        copy.start()
    for copy in copies:
        copy.wait()


def shards(
    ssm_input, dt_raw, b_proj, c_proj, dt_bias, decay_rate, skip_gain, doc_start, out_weight, grad_out
):
    rows, inner = ssm_input.shape
    heads = dt_raw.shape[1]
    state = b_proj.shape[2]
    n, nz = lax.axis_size("ctx"), lax.axis_size("tp")
    block, model = grad_out.shape
    columns = model // n
    dim, own = inner // heads, heads // n
    th, ht = (rows, heads), (heads, rows)
    V = pltpu.VMEM
    dma = pltpu.SemaphoreType.DMA
    vmem = pl.BlockSpec(memory_space=pltpu.VMEM)
    results = pl.pallas_call(
        mixer_kernel,
        out_shape=[
            jax.ShapeDtypeStruct(shape, kind)
            for shape, kind in (
                ((block, model), BF16), ((rows, inner), BF16), (ht, F32),
                ((rows, state), BF16), ((rows, state), BF16), ((columns, inner), BF16),
            )
        ],
        in_specs=[vmem] * 9 + [pl.BlockSpec(memory_space=pl.ANY)],
        out_specs=[vmem] * 5 + [pl.BlockSpec(memory_space=pl.ANY)],
        scratch_shapes=[
            V((inner, model), BF16), V((nz, block, model), BF16), V((nz, block, model), BF16),
            V((2, nz - 1, block, model), BF16), V((n, rows, inner), BF16),
            V((n, nz, block, columns), BF16),
            V((heads, dim + 16, state), BF16), V((n, own, dim + 16, state), BF16),
            V((n, own, dim, state), BF16), V((heads, dim, state), BF16),
            V((heads, dim, state), BF16), V((n, own, dim, state), BF16),
            V((n, own, dim, state), BF16), V((heads, dim, state), BF16),
            V(th, F32), V(ht, F32), V(th, F32), V(ht, F32), V(th, F32), V(th, F32),
            V((rows, rows), F32), V((rows, rows), F32),
            V((rows, inner), BF16), V((nz, block, inner), F32), V((columns, inner), F32), V((rows, inner), F32),
            V((3, rows, state), F32),
            V((3,) + th, F32), V(ht, F32), V((1, heads), F32),
            dma, dma((4, n)), dma((4, n)), dma((n,)), dma((n,)), dma((nz, 2, n)), dma((nz, 2, n)),
            dma((2, nz, 2)), dma((nz, 2)), dma((2, nz, 2)), dma((2, nz, 2)),
        ],
        compiler_params=pltpu.CompilerParams(
            collective_id=0, has_side_effects=True, vmem_limit_bytes=60 * 1024 * 1024
        ),
        name="mixer",
    )(
        ssm_input, dt_raw.T, b_proj.reshape(rows, state), c_proj.reshape(rows, state),
        dt_bias.reshape(1, heads), decay_rate.reshape(1, heads), skip_gain.reshape(1, heads),
        doc_start.reshape(1, rows), grad_out, out_weight,
    )
    anywhere = pl.BlockSpec(memory_space=pl.ANY)
    layer_out, dx, ddt, db, dc, weight_grad = pl.pallas_call(
        settle_kernel,
        out_shape=[jax.ShapeDtypeStruct(part.shape, part.dtype) for part in results],
        in_specs=[vmem] * 6,
        out_specs=[anywhere] * 6,
        scratch_shapes=[dma((6, 4))],
        compiler_params=pltpu.CompilerParams(vmem_limit_bytes=60 * 1024 * 1024),
        name="settle",
    )(*results)
    return (
        layer_out, dx, ddt.T, db.reshape(rows, 1, state), dc.reshape(rows, 1, state), weight_grad,
    )


def solution(mesh):
    in_specs = (
        P("ctx", "tp"), P("ctx", "tp"), P("ctx", "tp", None), P("ctx", "tp", None),
        P("tp"), P("tp"), P("tp"), P("ctx"), P("tp", None), P(("ctx", "tp"), None),
    )
    out_specs = (
        P(("ctx", "tp"), None), P("ctx", "tp"), P("ctx", "tp"),
        P("ctx", "tp", None), P("ctx", "tp", None), P("ctx", "tp"),
    )
    return jax.shard_map(shards, mesh=mesh, in_specs=in_specs, out_specs=out_specs, check_vma=False)
```
